256 devices in a mesh: section: 8 (over y, core), node: 32 (over z, x).
Axes of the slice: x: 4, y: 4, z: 8, core: 2. Of those that a mesh axis runs over, the one named last changes fastest.
Arguments:
- features_in: bfloat16 [8, 4096, 3, 256], P(None, 'node'), may hold values from -6 to 6
- filter_gate: bfloat16 [8, 2, 256, 512], P('section'), may hold values from -0.25 to 0.25
- self_mix: bfloat16 [8, 256, 256], P('section'), may hold values from -0.375 to 0.375
- hop_one_mix: bfloat16 [8, 2, 256, 256], P('section'), may hold values from -0.375 to 0.375
- hop_two_mix: bfloat16 [8, 2, 256, 256], P('section'), may hold values from -1 to 1
- skip_weight: bfloat16 [8, 256, 256], P('section'), may hold values from -0.375 to 0.375
- tile_values: bfloat16 [2, 32, 3, 128, 128], P(None, 'node'), may hold values from 0 to 0.125, as said below
- tile_columns: int32 [2, 32, 3], P(None, 'node'), may hold values from -1 to 32, as said below
- tile_counts: int32 [2, 32], P(None, 'node'), may hold values from 1 to 3
Outputs:
- skip_total: float32 [8, 32, 128, 3, 256], P(None, 'node', 'section')
The draws below stay inside these ranges and needn't reach their ends.
Inputs may be any that keep to these rules, and one draw needn't show every extreme that they name: `tile_columns`: for each direction and row block r the 3 slots name the blocks r - 1, r and r + 1, in an order drawn; -1 and 32 name no block. `tile_values`: entries are zero or positive.
All inputs are finite; a program needn't handle non-finite values.
Results may differ from the reference program's by a relative error of at most 0.028.
Values may be sent and summed in bfloat16 or wider, within the bound.
A program may use at most 64 MiB of HBM per device.

```python
import jax
import jax.numpy as jnp
from jax import lax

CHANNELS = 256
SKIP = 256
TILE = 128
SLOTS = 3
T_LEN = 3
MICRO = 8
LAYERS = 8
BLOCKS = 32
NODES = 4096


def draw_tile_values(key, part):
    first_key, second_key = jax.random.split(key)
    shape = (2, BLOCKS, SLOTS, TILE, TILE)
    keeper = (jax.random.randint(first_key, shape, 0, TILE) < 8).astype(jnp.float32)
    values = jax.random.uniform(second_key, shape, jnp.float32, 0.0, 0.125)
    return (values * keeper).astype(jnp.bfloat16)


def draw_tile_columns(key, part):
    scores = jax.random.randint(key, (2, BLOCKS, SLOTS), 0, 1 << 20) * SLOTS + jnp.arange(SLOTS, dtype=jnp.int32)
    ordering = jnp.argsort(scores, axis=-1).astype(jnp.int32)
    row_ids = jnp.arange(BLOCKS, dtype=jnp.int32)[None, :, None]
    return (row_ids + ordering - 1).astype(jnp.int32)


def set_ends(entries, own_key, smallest, high):
    longest = entries.shape.index(max(entries.shape))
    spots = []
    for shift in (0, 1):
        where = [jax.random.randint(jax.random.fold_in(own_key, axis), (), 0, length) for axis, length in enumerate(entries.shape)]
        where[longest] = (where[longest] + shift) % entries.shape[longest]
        spots.append(tuple(where))
    return entries.at[spots[0]].set(smallest).at[spots[1]].set(high)


def levels(own_key, dims, cuts, least, high):
    loudness, own = 1.0, jax.random.fold_in(own_key, 6)
    for dim, parts in cuts:
        draws = jnp.exp(jax.random.uniform(jax.random.fold_in(own, dim), (parts,), jnp.float32, least / len(cuts), high / len(cuts)))
        loudness = loudness * jnp.repeat(draws, dims[dim] // parts).reshape([-1 if axis == dim else 1 for axis in range(len(dims))])
    return loudness


def scatter_about(key, dims, scale, limit, cuts=(), held_as=jnp.bfloat16):
    loudness = levels(key, dims, cuts, -0.22, 0.18) if cuts else 1.0
    values = jax.random.normal(key, dims, jnp.float32) * scale * loudness
    return jnp.minimum(jnp.maximum(values, -limit), limit).astype(held_as)


def setup_inputs(seed: int = 0) -> dict:
    splits = jax.random.split(jax.random.key(seed), 10)
    features_in = scatter_about(splits[0], (MICRO, NODES, T_LEN, CHANNELS), 1.0, 6.0, ((1, 32),))
    filter_gate = scatter_about(splits[1], (LAYERS, 2, CHANNELS, 2 * CHANNELS), (2 * CHANNELS) ** -0.5, 0.25, ((0, 8),))
    self_mix = scatter_about(splits[2], (LAYERS, CHANNELS, CHANNELS), CHANNELS ** -0.5, 0.375, ((0, 8),))
    hop_one_mix = scatter_about(splits[3], (LAYERS, 2, CHANNELS, CHANNELS), CHANNELS ** -0.5, 0.375, ((0, 8),))
    hop_two_mix = scatter_about(splits[4], (LAYERS, 2, CHANNELS, CHANNELS), (CHANNELS // 8) ** -0.5, 1.0, ((0, 8),))
    skip_weight = scatter_about(splits[5], (LAYERS, CHANNELS, SKIP), CHANNELS ** -0.5, 0.375, ((0, 8),))
    tile_values = draw_tile_values(jax.random.fold_in(splits[9], 71), 0)
    tile_columns = draw_tile_columns(jax.random.fold_in(splits[9], 71), 0)
    tile_counts = set_ends(jax.random.randint(splits[8], (2, BLOCKS), 1, SLOTS + 1), jax.random.fold_in(splits[8], 1), 1, SLOTS).astype(jnp.int32)
    return dict(features_in=features_in, filter_gate=filter_gate, self_mix=self_mix, hop_one_mix=hop_one_mix, hop_two_mix=hop_two_mix, skip_weight=skip_weight, tile_values=tile_values, tile_columns=tile_columns, tile_counts=tile_counts)


def diffuse(values, tile_set, columns, counts):
    padded = jnp.pad(values, ((1, 1), (0, 0), (0, 0)))
    picked = padded[columns + 1].astype(jnp.float32)
    slot_ids = jnp.arange(SLOTS, dtype=jnp.int32)
    live_mask = (slot_ids[None, :] < counts[:, None]).astype(jnp.float32)
    weighted = tile_set.astype(jnp.float32) * live_mask[:, :, None, None]
    return jnp.einsum("bsij,bsjw->biw", weighted, picked)


def one_layer(state, level, filter_gate, self_mix, hop_one_mix, hop_two_mix, skip_weight, tile_values, tile_columns, tile_counts):
    dilation = 1 + level % 2
    earlier = jnp.pad(state, ((0, 0), (dilation, 0), (0, 0)))[:, :T_LEN]
    pre_act = jnp.dot(earlier.reshape(-1, CHANNELS), filter_gate[level, 0], preferred_element_type=jnp.float32)
    pre_act = pre_act + jnp.dot(state.reshape(-1, CHANNELS), filter_gate[level, 1], preferred_element_type=jnp.float32)
    hidden = (jnp.tanh(pre_act[:, :CHANNELS]) * jax.nn.sigmoid(pre_act[:, CHANNELS:])).astype(jnp.bfloat16)
    blocked = hidden.reshape(BLOCKS, TILE, T_LEN * CHANNELS)
    mixed_sum = jnp.dot(hidden, self_mix[level], preferred_element_type=jnp.float32)
    for direction in range(2):
        first_hop = diffuse(blocked, tile_values[direction], tile_columns[direction], tile_counts[direction]).astype(jnp.bfloat16)
        second_hop = diffuse(first_hop, tile_values[direction], tile_columns[direction], tile_counts[direction]).astype(jnp.bfloat16)
        mixed_sum = mixed_sum + jnp.dot(first_hop.reshape(-1, CHANNELS), hop_one_mix[level, direction], preferred_element_type=jnp.float32)
        mixed_sum = mixed_sum + jnp.dot(second_hop.reshape(-1, CHANNELS), hop_two_mix[level, direction], preferred_element_type=jnp.float32)
    next_state = (state.astype(jnp.float32) + mixed_sum.reshape(state.shape)).astype(jnp.bfloat16)
    skip_term = jnp.dot(hidden, skip_weight[level], preferred_element_type=jnp.float32)
    return next_state, skip_term


def reference(features_in, filter_gate, self_mix, hop_one_mix, hop_two_mix, skip_weight, tile_values, tile_columns, tile_counts):
    def run_sample(sample):
        state = sample
        total = jnp.zeros((NODES * T_LEN, SKIP), jnp.float32)
        for level in range(LAYERS):
            state, skip_term = one_layer(state, level, filter_gate, self_mix, hop_one_mix, hop_two_mix, skip_weight, tile_values, tile_columns, tile_counts)
            total = total + skip_term
        return total.reshape(BLOCKS, TILE, T_LEN, SKIP)

    return lax.map(run_sample, features_in)
```

```python
import jax
import jax.numpy as jnp
from jax import lax
from jax.sharding import PartitionSpec as P

F32 = jnp.float32
BF16 = jnp.bfloat16


def moved(value, steps):
    count = lax.axis_size("node")
    first, last = (max(0, -steps), min(count, count - steps))
    return lax.ppermute(value, "node", [(source, source + steps) for source in range(first, last)])


def body(
    features_in,
    filter_gate,
    self_mix,
    hop_one_mix,
    hop_two_mix,
    skip_weight,
    tile_values,
    tile_columns,
    tile_counts,
):
    micro, rows, steps_len, channels = features_in.shape
    width = steps_len * channels
    section_index = lax.axis_index("section")
    block_index = lax.axis_index("node")

    conv_all = lax.all_gather(filter_gate.reshape(1, 2 * channels, -1), "section", tiled=True)
    mixes = jnp.concatenate(
        [self_mix[:, None], hop_one_mix, hop_two_mix, skip_weight[:, None]], axis=1
    ).reshape(1, 6 * channels, -1)
    mix_all = lax.all_gather(mixes, "section", tiled=True)

    slot_ids = jnp.arange(tile_values.shape[2], dtype=jnp.int32)
    live = slot_ids[None, :] < tile_counts[:, 0][:, None]
    place = tile_columns[:, 0] - block_index + 1
    onehot = ((place[:, None, :] == jnp.arange(3)[None, :, None]) & live[:, None, :]).astype(BF16)
    near = jnp.einsum("dks,dsij->dikj", onehot, tile_values[:, 0]).astype(BF16)
    near = near.reshape(2, rows, 3 * rows)
    below, above = moved(near, 1), moved(near, -1)
    pad = lambda value, low, high: jnp.pad(value, ((0, 0), (0, 0), (low * rows, high * rows)))
    stacked = jnp.concatenate([pad(below, 0, 2), pad(near, 1, 1), pad(above, 2, 0)], axis=1)
    squared = jnp.einsum("dij,djk->dik", near, stacked, preferred_element_type=F32).astype(BF16)
    hops = jnp.concatenate([pad(near, 1, 1), squared], axis=0).reshape(4 * rows, 5 * rows)

    state = lax.dynamic_index_in_dim(features_in, section_index, 0, keepdims=False)
    state = state.transpose(1, 0, 2)
    layers = conv_all.shape[0]
    total = jnp.zeros((steps_len * rows, channels), F32)
    for layer in range(layers):
        back = 1 + layer % 2
        earlier = jnp.pad(state, ((back, 0), (0, 0), (0, 0)))[:steps_len]
        both = jnp.concatenate([earlier, state], axis=2).reshape(-1, 2 * channels)
        pre_act = jnp.dot(both, conv_all[layer], preferred_element_type=F32)
        hidden = (jnp.tanh(pre_act[:, :channels]) * jax.nn.sigmoid(pre_act[:, channels:])).astype(BF16)
        total = total + jnp.dot(hidden, mix_all[layer, 5 * channels :], preferred_element_type=F32)
        if layer == layers - 1:
            break
        fields = hidden.reshape(steps_len, rows, channels)
        window = jnp.concatenate(
            [moved(fields, 2), moved(fields, 1), fields, moved(fields, -1), moved(fields, -2)], axis=1
        )
        hopped = jnp.einsum("ij,tjc->tic", hops, window, preferred_element_type=F32).astype(BF16)
        hopped = hopped.reshape(steps_len, 4, rows, channels)
        mix = mix_all[layer]
        mixed = jnp.dot(hidden, mix[:channels], preferred_element_type=F32)
        for k in range(4):
            mixed = mixed + jnp.dot(
                hopped[:, k].reshape(-1, channels),
                mix[(1 + k) * channels : (2 + k) * channels],
                preferred_element_type=F32,
            )
        state = (state.astype(F32) + mixed.reshape(state.shape)).astype(BF16)
    out = total.reshape(steps_len, rows, channels).transpose(1, 0, 2)
    parts = lax.all_to_all(
        out.reshape(lax.axis_size("section"), -1, steps_len, channels), "section", 0, 0, tiled=True
    )
    return parts[:, None]


def solution(mesh):
    in_specs = (
        P(None, "node", None, None),
        P("section", None, None, None),
        P("section", None, None),
        P("section", None, None, None),
        P("section", None, None, None),
        P("section", None, None),
        P(None, "node", None, None, None),
        P(None, "node", None),
        P(None, "node"),
    )
    out_specs = P(None, "node", "section", None, None)
    return jax.shard_map(body, mesh=mesh, in_specs=in_specs, out_specs=out_specs, check_vma=False)
```

```python
import functools

import jax
import jax.numpy as jnp
from jax import lax
from jax.experimental import pallas as pl
from jax.experimental.pallas import tpu as pltpu
from jax.sharding import PartitionSpec as P

F32 = jnp.float32
BF16 = jnp.bfloat16
MESH = pl.DeviceIdType.MESH
XS = 4
YS = 4
LOOK = 6


def both(*conds):
    out = conds[0]
    for cond in conds[1:]:
        out = jnp.logical_and(out, cond)
    return out


def kernel(
    layers,
    blocks,
    feat,
    conv_in,
    self_in,
    one_in,
    two_in,
    skip_in,
    tiles,
    columns,
    counts,
    out,
    xs,
    hb,
    wc,
    wm,
    near,
    rows,
    hops,
    base,
    tot,
    obuf,
    load_sem,
    feat_sem,
    tile_send,
    tile_recv,
    halo_send,
    halo_recv,
    w_send,
    w_recv,
    w_sib,
    out_send,
    out_recv,
):
    steps, tile, ch = feat.shape
    last_layer = layers - 1
    s = lax.axis_index("section")
    n = lax.axis_index("node")
    y, c = lax.div(s, 2), lax.rem(s, 2)
    z, x = lax.div(n, XS), lax.rem(n, XS)
    last = blocks // 2 - 1

    group = lax.rem(lax.div(x + 1, 2), 2)
    side = lax.div(x, 2)
    place = side + lax.rem(z, 2) * (1 - 2 * side)
    k = 2 * z + place
    r = 2 * k + c
    m = 2 * y + group

    def node_at(group, k):
        z, place = lax.div(k, 2), lax.rem(k, 2)
        side = place + lax.rem(z, 2) * (1 - 2 * place)
        return XS * z + group + side * (3 - 2 * group)

    def device(section, node):
        return {"section": section, "node": node}

    def worker(sample, block):
        return device(
            2 * lax.div(sample, 2) + lax.rem(block, 2), node_at(lax.rem(sample, 2), lax.div(block, 2))
        )

    def remote(src, dst, send, recv, dev):
        return pltpu.make_async_remote_copy(
            src_ref=src, dst_ref=dst, send_sem=send, recv_sem=recv, device_id=dev, device_id_type=MESH
        )

    sib = device(2 * y + 1 - c, n)
    right = device(2 * y, node_at(group, jnp.minimum(k + 1, last)))
    left = device(2 * y + 1, node_at(group, jnp.maximum(k - 1, 0)))
    has_right, has_left = k < last, k > 0
    outer_ok = jnp.where(c == 0, has_left, has_right)
    inner_ok = jnp.where(c == 0, has_right, has_left)
    outer_k = jnp.clip(k - 1 + 2 * c, 0, last)
    ring = [lax.rem(y + 1, YS), lax.rem(y + YS - 1, YS)]

    at_home = n == r
    native = both(s == m, at_home)
    mine_to = worker(s, n)
    mine_from = device(m, r)
    n_out = n + 2 * lax.rem(n, 2) - 1
    r_out = r - 1 + 2 * c
    out_slot = 2 * (1 - lax.rem(n, 2))
    out_valid = both(n_out >= 0, n_out < blocks)
    in_valid = both(r_out >= 0, r_out < blocks)
    outer_to = worker(s, jnp.clip(n_out, 0, blocks - 1))
    outer_from = device(m, jnp.clip(r_out, 0, blocks - 1))
    outer_native = both(s == m, n == r_out)

    loads = [
        pltpu.make_async_copy(conv_in, wc.at[s], load_sem.at[0]),
        pltpu.make_async_copy(skip_in, wm.at[s, pl.ds(0, 4)], load_sem.at[1]),
        pltpu.make_async_copy(self_in, wm.at[s, pl.ds(4, 4)], load_sem.at[2]),
        pltpu.make_async_copy(one_in, wm.at[s, pl.ds(8, 8)], load_sem.at[3]),
        pltpu.make_async_copy(two_in, wm.at[s, pl.ds(16, 8)], load_sem.at[4]),
    ]
    for load in loads:
        load.start()

    barrier = pltpu.get_barrier_semaphore()

    def greet(dev):
        pl.semaphore_signal(barrier, inc=1, device_id=dev, device_id_type=MESH)

    greet(sib)
    for near_y in ring:
        for core in range(2):
            greet(device(2 * near_y + core, n))

    @pl.when(outer_ok)
    def _():
        for core in range(2):
            greet(device(2 * y + core, node_at(group, outer_k)))

    @pl.when(jnp.logical_not(native))
    def _():
        greet(mine_from)

    @pl.when(both(in_valid, jnp.logical_not(outer_native)))
    def _():
        greet(outer_from)

    for sample in range(layers):
        @pl.when(jnp.logical_not(both(at_home, m == sample)))
        def _():
            greet(worker(sample, n))

    for e in range(2):
        for w in range(3):
            total = jnp.zeros((tile, tile), F32)
            for slot in range(3):
                weight = both(columns[e, slot] == n - 1 + w, slot < counts[e, 0]).astype(F32)
                total = total + tiles[e, slot].astype(F32) * weight
            near[e, :, w * tile : (w + 1) * tile] = total.astype(BF16)
    xs[0:2] = jnp.zeros((2, tile, ch), BF16)
    tot[...] = jnp.zeros_like(tot)

    @pl.when(jnp.logical_not(outer_ok))
    def _():
        rows[2 * c] = jnp.zeros((2, tile, 3 * tile), BF16)

        @pl.loop(0, last_layer)
        def _(layer):
            for t in range(steps):
                hb[layer, t, 3 * c] = jnp.zeros((tile, ch), BF16)
                hb[layer, t, 3 * c + 1] = jnp.zeros((tile, ch), BF16)

    @pl.when(jnp.logical_not(inner_ok))
    def _():
        @pl.loop(0, last_layer)
        def _(layer):
            for t in range(steps):
                hb[layer, t, 4 - 4 * c] = jnp.zeros((tile, ch), BF16)

    as_int = lambda cond: cond.astype(jnp.int32)
    expected = (
        1
        + 4
        + as_int(has_right)
        + as_int(has_left)
        + 1
        - as_int(native)
        + as_int(both(out_valid, jnp.logical_not(outer_native)))
        + layers
        - as_int(at_home)
    )
    pl.semaphore_wait(barrier, expected)
    for load in loads:
        load.wait()

    def piece(layer, part, first, count):
        if part == 0:
            return wc.at[layer, pl.ds(first, count)]
        return wm.at[layer, pl.ds(12 * (part - 1) + 3 * first, 3 * count)]

    def ring_copy(layer, part, d, core, slot):
        ref = piece(layer, part, 2 * d + core, 1)
        return remote(
            ref, ref, w_send.at[layer, part, d, slot], w_recv.at[layer, part, d], device(2 * ring[d] + core, n)
        )

    def sib_copy(layer, part, d, whole):
        ref = piece(layer, part, 2 * d, 2) if whole else piece(layer, part, 2 * d + c, 1)
        return remote(ref, ref, w_send.at[layer, part, d, 2], w_sib.at[layer, part, d], sib)

    def sib_wait(layer, part, d, whole):
        ref = piece(layer, part, 2 * d, 2) if whole else piece(layer, part, 2 * d + 1 - c, 1)
        remote(ref, ref, w_send.at[layer, part, d, 2], w_sib.at[layer, part, d], sib).wait_recv()

    def distance(layer, d):
        gap = y - lax.div(layer, 2) if d == 0 else lax.div(layer, 2) - y
        return lax.rem(gap + YS, YS)

    def wanted(layer, part):
        valid = both(layer >= 0, layer < layers)
        return both(valid, layer < last_layer) if part == 2 else valid

    def point(l, t):
        for d in range(2):
            for h in range(YS):
                at = t + LOOK - h
                part = at % 3
                layer_at = l + at // 3
                layer = jnp.clip(layer_at, 0, last_layer)
                here = both(wanted(layer_at, part), distance(layer, d) == h)
                if h == 0:
                    @pl.when(both(here, lax.rem(layer, 2) == c))
                    def _():
                        for core in range(2):
                            ring_copy(layer, part, d, core, core).start()
                        sib_copy(layer, part, d, True).start()
                else:
                    @pl.when(here)
                    def _():
                        ring_copy(layer, part, d, c, 0).wait_recv()
                        if h < YS - 1:
                            ring_copy(layer, part, d, c, 0).start()
                        sib_copy(layer, part, d, False).start()

    def need(layer, part):
        same = lax.div(layer, 2) == y

        @pl.when(jnp.logical_not(same))
        def _():
            for d in range(2):
                sib_wait(layer, part, d, False)

        @pl.when(both(same, lax.rem(layer, 2) != c))
        def _():
            for d in range(2):
                sib_wait(layer, part, d, True)

    def drain_weights(layer, part):
        for d in range(2):
            gap = distance(layer, d)

            @pl.when(both(gap == 0, lax.rem(layer, 2) == c))
            def _():
                for core in range(2):
                    ring_copy(layer, part, d, core, core).wait_send()
                sib_copy(layer, part, d, True).wait_send()

            @pl.when(both(gap > 0, gap < YS - 1))
            def _():
                ring_copy(layer, part, d, c, 0).wait_send()

            @pl.when(gap > 0)
            def _():
                sib_copy(layer, part, d, False).wait_send()

    feat_copy = remote(feat, xs.at[pl.ds(2, steps)], feat_sem.at[0], feat_sem.at[1], mine_to)
    feat_local = pltpu.make_async_copy(feat, xs.at[pl.ds(2, steps)], feat_sem.at[1])
    own_copy = remote(near, rows.at[1], tile_send.at[0], tile_recv.at[0], mine_to)
    own_local = pltpu.make_async_copy(near, rows.at[1], tile_recv.at[0])
    outer_copy = remote(near, rows.at[out_slot], tile_send.at[1], tile_recv.at[1], outer_to)
    outer_local = pltpu.make_async_copy(near, rows.at[2 * c], tile_recv.at[1])
    outer_land = remote(near, rows.at[2 * c], tile_send.at[1], tile_recv.at[1], outer_to)
    swap_copy = remote(rows.at[1], rows.at[2 * c], tile_send.at[2], tile_recv.at[2], sib)
    swap_land = remote(rows.at[1], rows.at[2 - 2 * c], tile_send.at[2], tile_recv.at[2], sib)

    point(-2, 0)

    @pl.when(native)
    def _():
        feat_local.start()
        own_local.start()

    @pl.when(jnp.logical_not(native))
    def _():
        feat_copy.start()
        own_copy.start()

    @pl.when(outer_native)
    def _():
        outer_local.start()

    @pl.when(both(out_valid, jnp.logical_not(outer_native)))
    def _():
        outer_copy.start()

    point(-2, 1)
    point(-2, 2)
    point(-1, 0)

    def halo(l, t, which):
        own = hb.at[l, t, 2]
        if which == 0:
            return remote(own, hb.at[l, t, c], halo_send.at[l, t, 0], halo_recv.at[l, t, c], right)
        if which == 1:
            return remote(own, hb.at[l, t, c + 3], halo_send.at[l, t, 1], halo_recv.at[l, t, c], left)
        if which == 2:
            return remote(own, hb.at[l, t, 1 + 2 * c], halo_send.at[l, t, 2], halo_recv.at[l, t, 2], sib)
        return remote(
            hb.at[l, t, 1 + 2 * c], hb.at[l, t, 4 * c], halo_send.at[l, t, 3], halo_recv.at[l, t, 3], sib
        )

    def landed(l, t, slot, which):
        ref = hb.at[l, t, slot]
        remote(ref, ref, halo_send.at[l, t, 3], halo_recv.at[l, t, which], sib).wait_recv()

    def send_halo(l, t):
        @pl.when(has_right)
        def _():
            halo(l, t, 0).start()

        @pl.when(has_left)
        def _():
            halo(l, t, 1).start()

        halo(l, t, 2).start()

    def convolve(l, t):
        now = xs[2 + t]
        before = xs[1 + t - lax.rem(l, 2)]
        pre = jnp.dot(
            jnp.concatenate([before, now], axis=1), wc[l].reshape(2 * ch, 2 * ch), preferred_element_type=F32
        )
        gate = 0.5 * jnp.tanh(0.5 * pre[:, ch:]) + 0.5
        hb[l, t, 2] = (jnp.tanh(pre[:, :ch]) * gate).astype(BF16)

    @pl.when(native)
    def _():
        feat_local.wait()

    @pl.when(jnp.logical_not(native))
    def _():
        feat_copy.wait_recv()

    need(0, 0)
    for t in range(steps):
        convolve(0, t)
        send_halo(0, t)

    @pl.when(native)
    def _():
        own_local.wait()

    @pl.when(jnp.logical_not(native))
    def _():
        own_copy.wait_recv()

    swap_copy.start()

    @pl.when(outer_native)
    def _():
        outer_local.wait()

    @pl.when(both(in_valid, jnp.logical_not(outer_native)))
    def _():
        outer_land.wait_recv()

    point(-1, 1)
    point(-1, 2)
    swap_land.wait_recv()
    for e in range(2):
        mid = rows[1, e]
        one = jnp.concatenate([jnp.zeros((tile, tile), BF16), mid, jnp.zeros((tile, tile), BF16)], axis=1)
        hops[e * tile : (e + 1) * tile, :] = one
        for col in range(5):
            total = jnp.zeros((tile, tile), F32)
            for via in range(3):
                if 0 <= col - via < 3:
                    total = total + jnp.dot(
                        mid[:, via * tile : (via + 1) * tile],
                        rows[via, e, :, (col - via) * tile : (col - via + 1) * tile],
                        preferred_element_type=F32,
                    )
            hops[(2 + e) * tile : (3 + e) * tile, col * tile : (col + 1) * tile] = total.astype(BF16)

    @pl.loop(0, last_layer)
    def _(l):
        need(l, 1)
        need(l, 2)
        own = hb[l, :, 2].reshape(steps * tile, ch)
        tot[...] += jnp.dot(own, wm[l, 0:4].reshape(ch, ch), preferred_element_type=F32)
        base[...] = xs[2:].reshape(steps * tile, ch).astype(F32) + jnp.dot(
            own, wm[l, 4:8].reshape(ch, ch), preferred_element_type=F32
        )
        for t in range(steps):
            @pl.when(outer_ok)
            def _():
                landed(l, t, 1 + 2 * c, 1 - c)
                halo(l, t, 3).start()
                landed(l, t, 4 * c, c)

            point(l, t)
            landed(l, t, 3 - 2 * c, 2)

            @pl.when(inner_ok)
            def _():
                landed(l, t, 4 - 4 * c, 3)

            fields = jnp.dot(hops[...], hb[l, t].reshape(5 * tile, ch), preferred_element_type=F32).astype(BF16)
            wide = jnp.concatenate([fields[i * tile : (i + 1) * tile] for i in range(4)], axis=1)
            mixed = base[t * tile : (t + 1) * tile] + jnp.dot(
                wide, wm[l, 8:24].reshape(4 * ch, ch), preferred_element_type=F32
            )
            xs[2 + t] = mixed.astype(BF16)
            if t == 0:
                need(l + 1, 0)
            convolve(l + 1, t)

            @pl.when(l < last_layer - 1)
            def _():
                send_halo(l + 1, t)

    need(last_layer, 1)
    own = hb[last_layer, :, 2].reshape(steps * tile, ch)
    result = tot[...] + jnp.dot(own, wm[last_layer, 0:4].reshape(ch, ch), preferred_element_type=F32)
    obuf[...] = result.astype(BF16).reshape(obuf.shape)

    def out_copy(section):
        return remote(obuf.at[:, section], out.at[m], out_send.at[section], out_recv.at[m], device(section, r))

    def out_local(section):
        return pltpu.make_async_copy(obuf.at[:, section], out.at[m], out_recv.at[m])

    for section in range(layers):
        keep = both(at_home, s == section)

        @pl.when(keep)
        def _():
            out_local(section).start()

        @pl.when(jnp.logical_not(keep))
        def _():
            out_copy(section).start()

    @pl.when(jnp.logical_not(native))
    def _():
        feat_copy.wait_send()
        own_copy.wait_send()

    @pl.when(both(out_valid, jnp.logical_not(outer_native)))
    def _():
        outer_copy.wait_send()

    swap_copy.wait_send()

    @pl.loop(0, last_layer)
    def _(l):
        for t in range(steps):
            @pl.when(has_right)
            def _():
                halo(l, t, 0).wait_send()

            @pl.when(has_left)
            def _():
                halo(l, t, 1).wait_send()

            halo(l, t, 2).wait_send()

            @pl.when(outer_ok)
            def _():
                halo(l, t, 3).wait_send()

        for part in range(3):
            drain_weights(l, part)

    for part in range(2):
        drain_weights(last_layer, part)

    for section in range(layers):
        @pl.when(jnp.logical_not(both(at_home, s == section)))
        def _():
            out_copy(section).wait_send()

    for sample in range(layers):
        keep = both(at_home, m == sample)
        ref = out.at[sample]

        @pl.when(keep)
        def _():
            pltpu.make_async_copy(obuf.at[:, sample], ref, out_recv.at[sample]).wait()

        @pl.when(jnp.logical_not(keep))
        def _():
            remote(obuf.at[:, sample], ref, out_send.at[sample], out_recv.at[sample], sib).wait_recv()


def body(
    features_in,
    filter_gate,
    self_mix,
    hop_one_mix,
    hop_two_mix,
    skip_weight,
    tile_values,
    tile_columns,
    tile_counts,
):
    micro, tile, steps, ch = features_in.shape
    layers = lax.axis_size("section")
    blocks = lax.axis_size("node")
    part = ch // 4
    feat = lax.dynamic_index_in_dim(features_in, lax.axis_index("section"), 0, keepdims=False)
    feat = feat.transpose(1, 0, 2)
    dma = pltpu.SemaphoreType.DMA
    anywhere = pl.BlockSpec(memory_space=pl.ANY)
    in_vmem = pl.BlockSpec(memory_space=pltpu.VMEM)
    in_smem = pl.BlockSpec(memory_space=pltpu.SMEM)
    landed = pl.pallas_call(
        functools.partial(kernel, layers, blocks),
        out_shape=jax.ShapeDtypeStruct((micro, steps, tile // layers, ch), BF16),
        in_specs=[anywhere] * 6 + [in_vmem, in_smem, in_smem],
        out_specs=anywhere,
        scratch_shapes=[
            pltpu.VMEM((2 + steps, tile, ch), BF16),
            pltpu.VMEM((layers, steps, 5, tile, ch), BF16),
            pltpu.VMEM((layers, 4, ch // 2, 2 * ch), BF16),
            pltpu.VMEM((layers, 24, part, ch), BF16),
            pltpu.VMEM((2, tile, 3 * tile), BF16),
            pltpu.VMEM((3, 2, tile, 3 * tile), BF16),
            pltpu.VMEM((4 * tile, 5 * tile), BF16),
            pltpu.VMEM((steps * tile, ch), F32),
            pltpu.VMEM((steps * tile, ch), F32),
            pltpu.VMEM((steps, layers, tile // layers, ch), BF16),
            dma((5,)),
            dma((2,)),
            dma((3,)),
            dma((3,)),
            dma((layers - 1, steps, 4)),
            dma((layers - 1, steps, 4)),
            dma((layers, 3, 2, 3)),
            dma((layers, 3, 2)),
            dma((layers, 3, 2)),
            dma((layers,)),
            dma((layers,)),
        ],
        compiler_params=pltpu.CompilerParams(
            collective_id=0, has_side_effects=True, vmem_limit_bytes=44 * 1024 * 1024
        ),
        cost_estimate=pl.CostEstimate(flops=7_000_000_000, bytes_accessed=4_000_000, transcendentals=3_000_000),
    )(
        feat,
        filter_gate.reshape(4, ch // 2, 2 * ch),
        self_mix.reshape(4, part, ch),
        hop_one_mix.reshape(8, part, ch),
        hop_two_mix.reshape(8, part, ch),
        skip_weight.reshape(4, part, ch),
        tile_values[:, 0],
        tile_columns[:, 0],
        tile_counts,
    )
    return landed.transpose(0, 2, 1, 3).astype(F32)[:, None]


def solution(mesh):
    in_specs = (
        P(None, "node", None, None),
        P("section", None, None, None),
        P("section", None, None),
        P("section", None, None, None),
        P("section", None, None, None),
        P("section", None, None),
        P(None, "node", None, None, None),
        P(None, "node", None),
        P(None, "node"),
    )
    out_specs = P(None, "node", "section", None, None)
    return jax.shard_map(body, mesh=mesh, in_specs=in_specs, out_specs=out_specs, check_vma=False)
```

```python
import functools

import jax
import jax.numpy as jnp
from jax import lax
from jax.experimental import pallas as pl
from jax.experimental.pallas import tpu as pltpu
from jax.sharding import PartitionSpec as P

F32 = jnp.float32
BF16 = jnp.bfloat16
MESH = pl.DeviceIdType.MESH
XS = 4
YS = 4
CONV_AHEAD = (14, 11, 6, 3)
MIX_AHEAD = (25, 18, 10, 5, 1)
START = max(CONV_AHEAD + MIX_AHEAD)


def both(*conds):
    out = conds[0]
    for cond in conds[1:]:
        out = jnp.logical_and(out, cond)
    return out


def kernel(
    layers,
    blocks,
    feat,
    conv_in,
    self_in,
    one_in,
    two_in,
    skip_in,
    tiles,
    columns,
    counts,
    out,
    xs,
    hb,
    wc,
    wm,
    near,
    rows,
    hops,
    base,
    tot,
    obuf,
    load_sem,
    feat_sem,
    tile_send,
    tile_recv,
    halo_send,
    halo_recv,
    w_send,
    w_recv,
    w_sib,
    w_side,
    w_sib_side,
    out_send,
    out_recv,
):
    _, steps, tile, ch = feat.shape
    last_layer = layers - 1
    s = lax.axis_index("section")
    n = lax.axis_index("node")
    y, c = lax.div(s, 2), lax.rem(s, 2)
    z, x = lax.div(n, XS), lax.rem(n, XS)
    last = blocks // 2 - 1

    group = lax.rem(lax.div(x + 1, 2), 2)
    side = lax.div(x, 2)
    place = side + lax.rem(z, 2) * (1 - 2 * side)
    k = 2 * z + place
    r = 2 * k + c
    m = 2 * y + group

    def node_at(group, k):
        z, place = lax.div(k, 2), lax.rem(k, 2)
        side = place + lax.rem(z, 2) * (1 - 2 * place)
        return XS * z + group + side * (3 - 2 * group)

    def device(section, node):
        return {"section": section, "node": node}

    def worker(sample, block):
        return device(
            2 * lax.div(sample, 2) + lax.rem(block, 2), node_at(lax.rem(sample, 2), lax.div(block, 2))
        )

    def remote(src, dst, send, recv, dev):
        return pltpu.make_async_remote_copy(
            src_ref=src, dst_ref=dst, send_sem=send, recv_sem=recv, device_id=dev, device_id_type=MESH
        )

    sib = device(2 * y + 1 - c, n)
    right = device(2 * y, node_at(group, jnp.minimum(k + 1, last)))
    left = device(2 * y + 1, node_at(group, jnp.maximum(k - 1, 0)))
    has_right, has_left = k < last, k > 0
    outer_ok = jnp.where(c == 0, has_left, has_right)
    inner_ok = jnp.where(c == 0, has_right, has_left)
    outer_k = jnp.clip(k - 1 + 2 * c, 0, last)
    ring = [lax.rem(y + 1, YS), lax.rem(y + YS - 1, YS)]
    column = lax.rem(x, 2)
    partner = device(s, n + 1 - 2 * column)

    at_home = n == r
    native = both(s == m, at_home)
    mine_to = worker(s, n)
    mine_from = device(m, r)
    n_out = n + 2 * lax.rem(n, 2) - 1
    r_out = r - 1 + 2 * c
    out_slot = 2 * (1 - lax.rem(n, 2))
    out_valid = both(n_out >= 0, n_out < blocks)
    in_valid = both(r_out >= 0, r_out < blocks)
    outer_to = worker(s, jnp.clip(n_out, 0, blocks - 1))
    outer_from = device(m, jnp.clip(r_out, 0, blocks - 1))
    outer_native = both(s == m, n == r_out)

    loads = [
        pltpu.make_async_copy(conv_in, wc.at[s], load_sem.at[0]),
        pltpu.make_async_copy(skip_in, wm.at[s, pl.ds(0, 4)], load_sem.at[1]),
        pltpu.make_async_copy(self_in, wm.at[s, pl.ds(4, 4)], load_sem.at[2]),
        pltpu.make_async_copy(one_in, wm.at[s, pl.ds(8, 8)], load_sem.at[3]),
        pltpu.make_async_copy(two_in, wm.at[s, pl.ds(16, 8)], load_sem.at[4]),
    ]
    for load in loads:
        load.start()

    barrier = pltpu.get_barrier_semaphore()

    def greet(dev):
        pl.semaphore_signal(barrier, inc=1, device_id=dev, device_id_type=MESH)

    greet(sib)
    greet(partner)
    for near_y in ring:
        for core in range(2):
            greet(device(2 * near_y + core, n))

    @pl.when(outer_ok)
    def _():
        for core in range(2):
            greet(device(2 * y + core, node_at(group, outer_k)))

    @pl.when(jnp.logical_not(native))
    def _():
        greet(mine_from)

    @pl.when(both(in_valid, jnp.logical_not(outer_native)))
    def _():
        greet(outer_from)

    for sample in range(layers):
        @pl.when(jnp.logical_not(both(at_home, m == sample)))
        def _():
            greet(worker(sample, n))

    for e in range(2):
        for w in range(3):
            total = jnp.zeros((tile, tile), F32)
            for slot in range(3):
                weight = both(columns[e, slot] == n - 1 + w, slot < counts[e, 0]).astype(F32)
                total = total + tiles[e, slot].astype(F32) * weight
            near[e, :, w * tile : (w + 1) * tile] = total.astype(BF16)
    xs[0:2] = jnp.zeros((2, tile, ch), BF16)
    tot[...] = jnp.zeros_like(tot)

    @pl.when(jnp.logical_not(outer_ok))
    def _():
        rows[2 * c] = jnp.zeros((2, tile, 3 * tile), BF16)

        @pl.loop(0, last_layer)
        def _(layer):
            for t in range(steps):
                hb[layer, t, 3 * c] = jnp.zeros((tile, ch), BF16)
                hb[layer, t, 3 * c + 1] = jnp.zeros((tile, ch), BF16)

    @pl.when(jnp.logical_not(inner_ok))
    def _():
        @pl.loop(0, last_layer)
        def _(layer):
            for t in range(steps):
                hb[layer, t, 4 - 4 * c] = jnp.zeros((tile, ch), BF16)

    as_int = lambda cond: cond.astype(jnp.int32)
    expected = (
        2
        + 4
        + as_int(has_right)
        + as_int(has_left)
        + 1
        - as_int(native)
        + as_int(both(out_valid, jnp.logical_not(outer_native)))
        + layers
        - as_int(at_home)
    )
    pl.semaphore_wait(barrier, expected)
    for load in loads:
        load.wait()

    def conv_part(layer, first, count):
        return wc.at[layer, pl.ds(first, count)]

    def mix_part(layer, first, count):
        return wm.at[layer, pl.ds(3 * first, 3 * count)]

    def share(layer, kind, d, core):
        return conv_part(layer, 2 * d + core, 1) if kind == 0 else mix_part(layer, 4 * d + 2 * core + column, 1)

    def ring_copy(layer, kind, d, core, slot):
        ref = share(layer, kind, d, core)
        return remote(
            ref, ref, w_send.at[layer, kind, d, slot], w_recv.at[layer, kind, d], device(2 * ring[d] + core, n)
        )

    def whole_copy(layer, kind, d):
        ref = conv_part(layer, 2 * d, 2) if kind == 0 else mix_part(layer, 4 * d, 4)
        return remote(ref, ref, w_send.at[layer, kind, d, 2], w_sib.at[layer, kind, d], sib)

    def sib_copy(layer, kind, d, core):
        ref = share(layer, kind, d, core)
        return remote(ref, ref, w_send.at[layer, kind, d, 2], w_sib.at[layer, kind, d], sib)

    def side_copy(layer, d, from_column):
        ref = mix_part(layer, 4 * d + 2 * c + from_column, 1)
        return remote(ref, ref, w_send.at[layer, 1, d, 1], w_side.at[layer, d], partner)

    def side_sib(layer, d, core):
        ref = mix_part(layer, 4 * d + 2 * core + 1 - column, 1)
        return remote(ref, ref, w_send.at[layer, 1, d, 3], w_sib_side.at[layer, d], sib)

    def distance(layer, d):
        gap = y - lax.div(layer, 2) if d == 0 else lax.div(layer, 2) - y
        return lax.rem(gap + YS, YS)

    def deal(layer, kind, h, d, valid):
        if h == YS:
            @pl.when(both(valid, distance(layer, d) > 0))
            def _():
                side_copy(layer, d, 1 - column).wait_recv()
                side_sib(layer, d, c).start()
        elif h == 0:
            @pl.when(both(valid, distance(layer, d) == 0, lax.rem(layer, 2) == c))
            def _():
                for core in range(2):
                    ring_copy(layer, kind, d, core, core).start()
                whole_copy(layer, kind, d).start()
        else:
            @pl.when(both(valid, distance(layer, d) == h))
            def _():
                ring_copy(layer, kind, d, c, 0).wait_recv()
                if h < YS - 1:
                    ring_copy(layer, kind, d, c, 0).start()
                if kind == 1:
                    side_copy(layer, d, column).start()
                sib_copy(layer, kind, d, c).start()

    events = [(kind, h, ahead) for kind, table in ((0, CONV_AHEAD), (1, MIX_AHEAD)) for h, ahead in enumerate(table)]
    events.sort(key=lambda event: (event[1] > 0, event[2]))

    def point(l, t):
        for kind, h, ahead in events:
            if (t + ahead) % 3 == 0:
                layer = l + (t + ahead) // 3
                for d in range(2):
                    deal(jnp.minimum(layer, last_layer), kind, h, d, layer <= last_layer)

    def before(first, stop):
        for step in range(first, stop):
            for kind, h, ahead in events:
                if (step + ahead) % 3 == 0 and 0 <= step + ahead < 3 * layers:
                    for d in range(2):
                        deal(jnp.int32((step + ahead) // 3), kind, h, d, jnp.bool_(True))

    def need(layer, kind):
        same = lax.div(layer, 2) == y

        @pl.when(jnp.logical_not(same))
        def _():
            for d in range(2):
                sib_copy(layer, kind, d, 1 - c).wait_recv()
                if kind == 1:
                    side_sib(layer, d, 1 - c).wait_recv()

        @pl.when(both(same, lax.rem(layer, 2) != c))
        def _():
            for d in range(2):
                whole_copy(layer, kind, d).wait_recv()

    def drain_weights(layer):
        for kind in range(2):
            for d in range(2):
                gap = distance(layer, d)

                @pl.when(both(gap == 0, lax.rem(layer, 2) == c))
                def _():
                    for core in range(2):
                        ring_copy(layer, kind, d, core, core).wait_send()
                    whole_copy(layer, kind, d).wait_send()

                @pl.when(both(gap > 0, gap < YS - 1))
                def _():
                    ring_copy(layer, kind, d, c, 0).wait_send()

                @pl.when(gap > 0)
                def _():
                    sib_copy(layer, kind, d, c).wait_send()
                    if kind == 1:
                        side_copy(layer, d, column).wait_send()
                        side_sib(layer, d, c).wait_send()

    mine = feat.at[s]
    feat_copy = remote(mine, xs.at[pl.ds(2, steps)], feat_sem.at[0], feat_sem.at[1], mine_to)
    feat_local = pltpu.make_async_copy(mine, xs.at[pl.ds(2, steps)], feat_sem.at[1])
    own_copy = remote(near, rows.at[1], tile_send.at[0], tile_recv.at[0], mine_to)
    own_local = pltpu.make_async_copy(near, rows.at[1], tile_recv.at[0])
    outer_copy = remote(near, rows.at[out_slot], tile_send.at[1], tile_recv.at[1], outer_to)
    outer_local = pltpu.make_async_copy(near, rows.at[2 * c], tile_recv.at[1])
    outer_land = remote(near, rows.at[2 * c], tile_send.at[1], tile_recv.at[1], outer_to)
    swap_copy = remote(rows.at[1], rows.at[2 * c], tile_send.at[2], tile_recv.at[2], sib)
    swap_land = remote(rows.at[1], rows.at[2 - 2 * c], tile_send.at[2], tile_recv.at[2], sib)

    before(-START, 1 - CONV_AHEAD[0])

    @pl.when(native)
    def _():
        feat_local.start()
        own_local.start()

    @pl.when(jnp.logical_not(native))
    def _():
        feat_copy.start()
        own_copy.start()

    @pl.when(outer_native)
    def _():
        outer_local.start()

    @pl.when(both(out_valid, jnp.logical_not(outer_native)))
    def _():
        outer_copy.start()

    before(1 - CONV_AHEAD[0], 1 - CONV_AHEAD[3])

    def halo(l, t, which):
        own = hb.at[l, t, 2]
        if which == 0:
            return remote(own, hb.at[l, t, c], halo_send.at[l, t, 0], halo_recv.at[l, t, c], right)
        if which == 1:
            return remote(own, hb.at[l, t, c + 3], halo_send.at[l, t, 1], halo_recv.at[l, t, c], left)
        if which == 2:
            return remote(own, hb.at[l, t, 1 + 2 * c], halo_send.at[l, t, 2], halo_recv.at[l, t, 2], sib)
        return remote(
            hb.at[l, t, 1 + 2 * c], hb.at[l, t, 4 * c], halo_send.at[l, t, 3], halo_recv.at[l, t, 3], sib
        )

    def landed(l, t, slot, which):
        ref = hb.at[l, t, slot]
        remote(ref, ref, halo_send.at[l, t, 3], halo_recv.at[l, t, which], sib).wait_recv()

    def send_halo(l, t):
        @pl.when(has_right)
        def _():
            halo(l, t, 0).start()

        @pl.when(has_left)
        def _():
            halo(l, t, 1).start()

        halo(l, t, 2).start()

    def convolve(l, t):
        now = xs[2 + t]
        before = xs[1 + t - lax.rem(l, 2)]
        pre = jnp.dot(
            jnp.concatenate([before, now], axis=1), wc[l].reshape(2 * ch, 2 * ch), preferred_element_type=F32
        )
        gate = 0.5 * jnp.tanh(0.5 * pre[:, ch:]) + 0.5
        hb[l, t, 2] = (jnp.tanh(pre[:, :ch]) * gate).astype(BF16)

    @pl.when(native)
    def _():
        feat_local.wait()

    @pl.when(jnp.logical_not(native))
    def _():
        feat_copy.wait_recv()

    need(0, 0)
    for t in range(steps):
        convolve(0, t)
        send_halo(0, t)

    @pl.when(native)
    def _():
        own_local.wait()

    @pl.when(jnp.logical_not(native))
    def _():
        own_copy.wait_recv()

    swap_copy.start()

    @pl.when(outer_native)
    def _():
        outer_local.wait()

    @pl.when(both(in_valid, jnp.logical_not(outer_native)))
    def _():
        outer_land.wait_recv()

    before(1 - CONV_AHEAD[3], 0)
    swap_land.wait_recv()
    for e in range(2):
        mid = rows[1, e]
        one = jnp.concatenate([jnp.zeros((tile, tile), BF16), mid, jnp.zeros((tile, tile), BF16)], axis=1)
        hops[e * tile : (e + 1) * tile, :] = one
        for col in range(5):
            total = jnp.zeros((tile, tile), F32)
            for via in range(3):
                if 0 <= col - via < 3:
                    total = total + jnp.dot(
                        mid[:, via * tile : (via + 1) * tile],
                        rows[via, e, :, (col - via) * tile : (col - via + 1) * tile],
                        preferred_element_type=F32,
                    )
            hops[(2 + e) * tile : (3 + e) * tile, col * tile : (col + 1) * tile] = total.astype(BF16)

    @pl.loop(0, last_layer)
    def _(l):
        need(l, 1)
        own = hb[l, :, 2].reshape(steps * tile, ch)
        tot[...] += jnp.dot(own, wm[l, 0:4].reshape(ch, ch), preferred_element_type=F32)
        base[...] = xs[2:].reshape(steps * tile, ch).astype(F32) + jnp.dot(
            own, wm[l, 4:8].reshape(ch, ch), preferred_element_type=F32
        )
        for t in range(steps):
            @pl.when(outer_ok)
            def _():
                landed(l, t, 1 + 2 * c, 1 - c)
                halo(l, t, 3).start()
                landed(l, t, 4 * c, c)

            point(l, t)
            landed(l, t, 3 - 2 * c, 2)

            @pl.when(inner_ok)
            def _():
                landed(l, t, 4 - 4 * c, 3)

            fields = jnp.dot(hops[...], hb[l, t].reshape(5 * tile, ch), preferred_element_type=F32).astype(BF16)
            wide = jnp.concatenate([fields[i * tile : (i + 1) * tile] for i in range(4)], axis=1)
            mixed = base[t * tile : (t + 1) * tile] + jnp.dot(
                wide, wm[l, 8:24].reshape(4 * ch, ch), preferred_element_type=F32
            )
            xs[2 + t] = mixed.astype(BF16)
            if t == 0:
                need(l + 1, 0)
            convolve(l + 1, t)

            @pl.when(l < last_layer - 1)
            def _():
                send_halo(l + 1, t)

    need(last_layer, 1)
    own = hb[last_layer, :, 2].reshape(steps * tile, ch)
    result = tot[...] + jnp.dot(own, wm[last_layer, 0:4].reshape(ch, ch), preferred_element_type=F32)
    obuf[...] = result.astype(BF16).reshape(obuf.shape)

    def out_copy(section):
        return remote(obuf.at[:, section], out.at[m], out_send.at[section], out_recv.at[m], device(section, r))

    def out_local(section):
        return pltpu.make_async_copy(obuf.at[:, section], out.at[m], out_recv.at[m])

    for section in range(layers):
        keep = both(at_home, s == section)

        @pl.when(keep)
        def _():
            out_local(section).start()

        @pl.when(jnp.logical_not(keep))
        def _():
            out_copy(section).start()

    @pl.when(jnp.logical_not(native))
    def _():
        feat_copy.wait_send()
        own_copy.wait_send()

    @pl.when(both(out_valid, jnp.logical_not(outer_native)))
    def _():
        outer_copy.wait_send()

    swap_copy.wait_send()

    @pl.loop(0, last_layer)
    def _(l):
        for t in range(steps):
            @pl.when(has_right)
            def _():
                halo(l, t, 0).wait_send()

            @pl.when(has_left)
            def _():
                halo(l, t, 1).wait_send()

            halo(l, t, 2).wait_send()

            @pl.when(outer_ok)
            def _():
                halo(l, t, 3).wait_send()

        drain_weights(l)

    drain_weights(last_layer)

    for section in range(layers):
        @pl.when(jnp.logical_not(both(at_home, s == section)))
        def _():
            out_copy(section).wait_send()

    for sample in range(layers):
        keep = both(at_home, m == sample)
        ref = out.at[sample]

        @pl.when(keep)
        def _():
            pltpu.make_async_copy(obuf.at[:, sample], ref, out_recv.at[sample]).wait()

        @pl.when(jnp.logical_not(keep))
        def _():
            remote(obuf.at[:, sample], ref, out_send.at[sample], out_recv.at[sample], sib).wait_recv()


def body(
    features_in,
    filter_gate,
    self_mix,
    hop_one_mix,
    hop_two_mix,
    skip_weight,
    tile_values,
    tile_columns,
    tile_counts,
):
    micro, tile, steps, ch = features_in.shape
    layers = lax.axis_size("section")
    blocks = lax.axis_size("node")
    part = ch // 4
    feat = features_in.transpose(0, 2, 1, 3)
    dma = pltpu.SemaphoreType.DMA
    in_hbm = pl.BlockSpec(memory_space=pltpu.HBM)
    in_vmem = pl.BlockSpec(memory_space=pltpu.VMEM)
    in_smem = pl.BlockSpec(memory_space=pltpu.SMEM)
    landed = pl.pallas_call(
        functools.partial(kernel, layers, blocks),
        out_shape=jax.ShapeDtypeStruct((micro, steps, tile // layers, ch), BF16),
        in_specs=[in_hbm] * 6 + [in_vmem, in_smem, in_smem],
        out_specs=in_hbm,
        scratch_shapes=[
            pltpu.VMEM((2 + steps, tile, ch), BF16),
            pltpu.VMEM((layers, steps, 5, tile, ch), BF16),
            pltpu.VMEM((layers, 4, ch // 2, 2 * ch), BF16),
            pltpu.VMEM((layers, 24, part, ch), BF16),
            pltpu.VMEM((2, tile, 3 * tile), BF16),
            pltpu.VMEM((3, 2, tile, 3 * tile), BF16),
            pltpu.VMEM((4 * tile, 5 * tile), BF16),
            pltpu.VMEM((steps * tile, ch), F32),
            pltpu.VMEM((steps * tile, ch), F32),
            pltpu.VMEM((steps, layers, tile // layers, ch), BF16),
            dma((5,)),
            dma((2,)),
            dma((3,)),
            dma((3,)),
            dma((layers - 1, steps, 4)),
            dma((layers - 1, steps, 4)),
            dma((layers, 2, 2, 4)),
            dma((layers, 2, 2)),
            dma((layers, 2, 2)),
            dma((layers, 2)),
            dma((layers, 2)),
            dma((layers,)),
            dma((layers,)),
        ],
        compiler_params=pltpu.CompilerParams(
            collective_id=0, has_side_effects=True, vmem_limit_bytes=62 * 1024 * 1024
        ),
        cost_estimate=pl.CostEstimate(flops=7_000_000_000, bytes_accessed=4_000_000, transcendentals=3_000_000),
    )(
        feat,
        filter_gate.reshape(4, ch // 2, 2 * ch),
        self_mix.reshape(4, part, ch),
        hop_one_mix.reshape(8, part, ch),
        hop_two_mix.reshape(8, part, ch),
        skip_weight.reshape(4, part, ch),
        tile_values[:, 0],
        tile_columns[:, 0],
        tile_counts,
    )
    return landed.transpose(0, 2, 1, 3).astype(F32)[:, None]


def solution(mesh):
    in_specs = (
        P(None, "node", None, None),
        P("section", None, None, None),
        P("section", None, None),
        P("section", None, None, None),
        P("section", None, None, None),
        P("section", None, None),
        P(None, "node", None, None, None),
        P(None, "node", None),
        P(None, "node"),
    )
    out_specs = P(None, "node", "section", None, None)
    return jax.shard_map(body, mesh=mesh, in_specs=in_specs, out_specs=out_specs, check_vma=False)
```

```python
import functools

import jax
import jax.numpy as jnp
from jax import lax
from jax.experimental import pallas as pl
from jax.experimental.pallas import tpu as pltpu
from jax.sharding import PartitionSpec as P

F32 = jnp.float32
BF16 = jnp.bfloat16
MESH = pl.DeviceIdType.MESH
XS = 4
YS = 4
CONV_AHEAD = (15, 10, 4)
MIX_AHEAD = (15, 9, 3)
START = max(CONV_AHEAD + MIX_AHEAD)
SHARED = 8


def both(*conds):
    out = conds[0]
    for cond in conds[1:]:
        out = jnp.logical_and(out, cond)
    return out


def kernel(
    layers,
    blocks,
    feat,
    conv_in,
    self_in,
    one_in,
    two_in,
    skip_in,
    tiles,
    columns,
    counts,
    out,
    xs,
    hb,
    wc,
    wm,
    near,
    rows,
    hops,
    near_hops,
    far_hops,
    base,
    tot,
    obuf,
    load_sem,
    feat_sem,
    tile_send,
    tile_recv,
    plane_send,
    plane_recv,
    halo_send,
    halo_recv,
    w_send,
    w_recv,
    w_quad,
    w_sib,
    out_send,
    out_recv,
):
    _, steps, tile, ch = feat.shape
    last_layer = layers - 1
    s = lax.axis_index("section")
    n = lax.axis_index("node")
    y, c = lax.div(s, 2), lax.rem(s, 2)
    z, x = lax.div(n, XS), lax.rem(n, XS)
    last = blocks // 2 - 1

    group = lax.rem(lax.div(x + 1, 2), 2)
    side = lax.div(x, 2)
    place = side + lax.rem(z, 2) * (1 - 2 * side)
    k = 2 * z + place
    r = 2 * k + c
    m = 2 * y + group

    def node_at(group, k):
        z, place = lax.div(k, 2), lax.rem(k, 2)
        side = place + lax.rem(z, 2) * (1 - 2 * place)
        return XS * z + group + side * (3 - 2 * group)

    def device(section, node):
        return {"section": section, "node": node}

    def worker(sample, block):
        return device(
            2 * lax.div(sample, 2) + lax.rem(block, 2), node_at(lax.rem(sample, 2), lax.div(block, 2))
        )

    def remote(src, dst, send, recv, dev):
        return pltpu.make_async_remote_copy(
            src_ref=src, dst_ref=dst, send_sem=send, recv_sem=recv, device_id=dev, device_id_type=MESH
        )

    sib = device(2 * y + 1 - c, n)
    right = device(2 * y, node_at(group, jnp.minimum(k + 1, last)))
    left = device(2 * y + 1, node_at(group, jnp.maximum(k - 1, 0)))
    has_right, has_left = k < last, k > 0
    outer_ok = jnp.where(c == 0, has_left, has_right)
    inner_ok = jnp.where(c == 0, has_right, has_left)
    outer_k = jnp.clip(k - 1 + 2 * c, 0, last)

    zs = blocks // XS
    odd_x = lax.rem(x, 2)
    low_z = lax.rem(z + side, 2)
    quad = odd_x + 2 * low_z
    quad_x = x + 1 - 2 * odd_x
    quad_z = lax.rem(z + 1 - 2 * low_z + zs, zs)
    quad_devices = [device(s, XS * z + quad_x), device(s, XS * quad_z + x), device(s, XS * quad_z + quad_x)]
    flip_x, flip_z = 1 - 2 * odd_x, 2 - 4 * low_z
    quad_parts = [quad + flip_x, quad + flip_z, quad + flip_x + flip_z]

    at_home = n == r
    native = both(s == m, at_home)
    mine_to = worker(s, n)
    mine_from = device(m, r)
    n_out = n + 2 * lax.rem(n, 2) - 1
    r_out = r - 1 + 2 * c
    out_slot = 2 * (1 - lax.rem(n, 2))
    out_valid = both(n_out >= 0, n_out < blocks)
    in_valid = both(r_out >= 0, r_out < blocks)
    outer_to = worker(s, jnp.clip(n_out, 0, blocks - 1))
    outer_from = device(m, jnp.clip(r_out, 0, blocks - 1))
    outer_native = both(s == m, n == r_out)

    loads = [
        pltpu.make_async_copy(conv_in, wc.at[s], load_sem.at[0]),
        pltpu.make_async_copy(skip_in, wm.at[s, pl.ds(0, 4)], load_sem.at[1]),
        pltpu.make_async_copy(self_in, wm.at[s, pl.ds(4, 4)], load_sem.at[2]),
        pltpu.make_async_copy(one_in, wm.at[s, pl.ds(8, 8)], load_sem.at[3]),
        pltpu.make_async_copy(two_in, wm.at[s, pl.ds(16, 8)], load_sem.at[4]),
    ]
    for load in loads:
        load.start()

    barrier = pltpu.get_barrier_semaphore()

    def greet(dev):
        pl.semaphore_signal(barrier, inc=1, device_id=dev, device_id_type=MESH)

    greet(sib)
    for friend in quad_devices:
        greet(friend)
    for step in range(1, YS):
        for core in range(2):
            greet(device(2 * lax.rem(y + step, YS) + core, n))

    @pl.when(outer_ok)
    def _():
        for core in range(2):
            greet(device(2 * y + core, node_at(group, outer_k)))

    @pl.when(jnp.logical_not(native))
    def _():
        greet(mine_from)

    @pl.when(both(in_valid, jnp.logical_not(outer_native)))
    def _():
        greet(outer_from)

    for sample in range(layers):
        @pl.when(jnp.logical_not(both(at_home, m == sample)))
        def _():
            greet(worker(sample, n))

    for e in range(2):
        for w in range(3):
            total = jnp.zeros((tile, tile), F32)
            for slot in range(3):
                weight = both(columns[e, slot] == n - 1 + w, slot < counts[e, 0]).astype(F32)
                total = total + tiles[e, slot].astype(F32) * weight
            near[:, e, :, w * tile : (w + 1) * tile] = total.astype(BF16).reshape(YS, tile // YS, tile)
    xs[0:2] = jnp.zeros((2, tile, ch), BF16)
    tot[...] = jnp.zeros_like(tot)

    @pl.when(jnp.logical_not(outer_ok))
    def _():
        rows[2 * c] = jnp.zeros(near.shape, BF16)

        @pl.loop(0, last_layer)
        def _(layer):
            for t in range(steps):
                hb[layer, t, 3 * c] = jnp.zeros((tile, ch), BF16)
                hb[layer, t, 3 * c + 1] = jnp.zeros((tile, ch), BF16)

    @pl.when(jnp.logical_not(inner_ok))
    def _():
        @pl.loop(0, last_layer)
        def _(layer):
            for t in range(steps):
                hb[layer, t, 4 - 4 * c] = jnp.zeros((tile, ch), BF16)

    as_int = lambda cond: cond.astype(jnp.int32)
    expected = (
        1
        + 3
        + 2 * (YS - 1)
        + as_int(has_right)
        + as_int(has_left)
        + 1
        - as_int(native)
        + as_int(both(out_valid, jnp.logical_not(outer_native)))
        + layers
        - as_int(at_home)
    )
    pl.semaphore_wait(barrier, expected)
    for load in loads:
        load.wait()

    def piece(layer, kind, first, count):
        return wc.at[layer, pl.ds(first, count)] if kind == 0 else wm.at[layer, pl.ds(3 * first, 3 * count)]

    others = [lax.rem(y + step, YS) for step in range(1, YS)]

    def owner_copy(layer, kind, step, core, shared):
        ref = piece(layer, kind, 4 * core + quad, 1) if shared else piece(layer, kind, 4 * core, 4)
        return remote(
            ref,
            ref,
            w_send.at[layer, kind, 2 * step + core],
            w_recv.at[layer, kind],
            device(2 * others[step] + core, n),
        )

    def owner_land(layer, kind, shared):
        ref = piece(layer, kind, 4 * c + quad, 1) if shared else piece(layer, kind, 4 * c, 4)
        return remote(ref, ref, w_send.at[layer, kind, 0], w_recv.at[layer, kind], sib)

    def quad_copy(layer, kind, i):
        ref = piece(layer, kind, 4 * c + quad, 1)
        return remote(ref, ref, w_send.at[layer, kind, i], w_quad.at[layer, kind, i], quad_devices[i])

    def quad_land(layer, kind, i):
        ref = piece(layer, kind, 4 * c + quad_parts[i], 1)
        return remote(ref, ref, w_send.at[layer, kind, i], w_quad.at[layer, kind, i], sib)

    def whole_copy(layer, kind):
        ref = piece(layer, kind, 0, 8)
        return remote(ref, ref, w_send.at[layer, kind, 6], w_sib.at[layer, kind], sib)

    def half_copy(layer, kind, core):
        ref = piece(layer, kind, 4 * core, 4)
        return remote(ref, ref, w_send.at[layer, kind, 6], w_sib.at[layer, kind], sib)

    def deal(layer, kind, stage, valid):
        same = lax.div(layer, 2) == y
        apart = both(valid, jnp.logical_not(same))
        early = layer < SHARED
        late = jnp.logical_not(early)
        if stage == 0:
            mine = both(valid, same, lax.rem(layer, 2) == c)
            for shared, when in ((True, early), (False, late)):
                @pl.when(both(mine, when))
                def _():
                    for step in (1, 0, 2):
                        for core in range(2):
                            owner_copy(layer, kind, step, core, shared).start()

            @pl.when(mine)
            def _():
                whole_copy(layer, kind).start()
        elif stage == 1:
            @pl.when(both(apart, early))
            def _():
                owner_land(layer, kind, True).wait_recv()
                for i in (2, 0, 1):
                    quad_copy(layer, kind, i).start()

            @pl.when(both(apart, late))
            def _():
                owner_land(layer, kind, False).wait_recv()
                half_copy(layer, kind, c).start()
        else:
            @pl.when(both(apart, early))
            def _():
                for i in range(3):
                    quad_land(layer, kind, i).wait_recv()
                half_copy(layer, kind, c).start()

    events = [
        (kind, stage, ahead) for kind, table in ((0, CONV_AHEAD), (1, MIX_AHEAD)) for stage, ahead in enumerate(table)
    ]
    events.sort(key=lambda event: (event[1] > 0, event[2]))

    def point(l, t):
        for kind, stage, ahead in events:
            if (t + ahead) % 3 == 0:
                layer = l + (t + ahead) // 3
                deal(jnp.minimum(layer, last_layer), kind, stage, layer <= last_layer)

    def before(first, stop):
        for step in range(first, stop):
            for kind, stage, ahead in events:
                if (step + ahead) % 3 == 0 and 0 <= step + ahead < 3 * layers:
                    deal(jnp.int32((step + ahead) // 3), kind, stage, jnp.bool_(True))

    def need(layer, kind):
        same = lax.div(layer, 2) == y

        @pl.when(jnp.logical_not(same))
        def _():
            half_copy(layer, kind, 1 - c).wait_recv()

        @pl.when(both(same, lax.rem(layer, 2) != c))
        def _():
            whole_copy(layer, kind).wait_recv()

    def drain_weights(layer):
        same = lax.div(layer, 2) == y
        early = layer < SHARED
        for kind in range(2):
            for shared, when in ((True, early), (False, jnp.logical_not(early))):
                @pl.when(both(same, lax.rem(layer, 2) == c, when))
                def _():
                    for step in range(YS - 1):
                        for core in range(2):
                            owner_copy(layer, kind, step, core, shared).wait_send()

            @pl.when(both(same, lax.rem(layer, 2) == c))
            def _():
                whole_copy(layer, kind).wait_send()

            @pl.when(both(jnp.logical_not(same), early))
            def _():
                for i in range(3):
                    quad_copy(layer, kind, i).wait_send()

            @pl.when(jnp.logical_not(same))
            def _():
                half_copy(layer, kind, c).wait_send()

    mine = feat.at[s]
    feat_copy = remote(mine, xs.at[pl.ds(2, steps)], feat_sem.at[0], feat_sem.at[1], mine_to)
    feat_local = pltpu.make_async_copy(mine, xs.at[pl.ds(2, steps)], feat_sem.at[1])
    own_copy = remote(near.at[y], rows.at[1, y], tile_send.at[0], tile_recv.at[0], mine_to)
    own_local = pltpu.make_async_copy(near, rows.at[1], tile_recv.at[0])
    outer_copy = remote(near.at[y], rows.at[out_slot, y], tile_send.at[1], tile_recv.at[1], outer_to)
    outer_local = pltpu.make_async_copy(near, rows.at[2 * c], tile_recv.at[1])
    outer_land = remote(near.at[y], rows.at[2 * c, y], tile_send.at[1], tile_recv.at[1], outer_to)
    swap_copy = remote(rows.at[1], rows.at[2 * c], tile_send.at[2], tile_recv.at[2], sib)
    def plane_copy(slot, which, step):
        ref = rows.at[slot, y]
        return remote(
            ref, ref, plane_send.at[which, step], plane_recv.at[which, step], device(2 * others[step] + c, n)
        )

    def plane_land(slot, which, step):
        ref = rows.at[slot, others[YS - 2 - step]]
        return remote(ref, ref, plane_send.at[which, step], plane_recv.at[which, step], sib)

    swap_land = remote(rows.at[1], rows.at[2 - 2 * c], tile_send.at[2], tile_recv.at[2], sib)

    before(-START, 1 - CONV_AHEAD[0])

    @pl.when(native)
    def _():
        feat_local.start()
        own_local.start()

    @pl.when(jnp.logical_not(native))
    def _():
        feat_copy.start()
        own_copy.start()

    @pl.when(outer_native)
    def _():
        outer_local.start()

    @pl.when(both(out_valid, jnp.logical_not(outer_native)))
    def _():
        outer_copy.start()

    before(1 - CONV_AHEAD[0], 1 - CONV_AHEAD[1])

    @pl.when(jnp.logical_not(native))
    def _():
        own_copy.wait_recv()
        for step in range(YS - 1):
            plane_copy(1, 0, step).start()

    @pl.when(both(in_valid, jnp.logical_not(outer_native)))
    def _():
        outer_land.wait_recv()
        for step in range(YS - 1):
            plane_copy(2 * c, 1, step).start()

    before(1 - CONV_AHEAD[1], 1 - CONV_AHEAD[2])

    def halo(l, t, which):
        own = hb.at[l, t, 2]
        if which == 0:
            return remote(own, hb.at[l, t, c], halo_send.at[l, t, 0], halo_recv.at[l, t, c], right)
        if which == 1:
            return remote(own, hb.at[l, t, c + 3], halo_send.at[l, t, 1], halo_recv.at[l, t, c], left)
        if which == 2:
            return remote(own, hb.at[l, t, 1 + 2 * c], halo_send.at[l, t, 2], halo_recv.at[l, t, 2], sib)
        return remote(
            hb.at[l, t, 1 + 2 * c], hb.at[l, t, 4 * c], halo_send.at[l, t, 3], halo_recv.at[l, t, 3], sib
        )

    def landed(l, t, slot, which):
        ref = hb.at[l, t, slot]
        remote(ref, ref, halo_send.at[l, t, 3], halo_recv.at[l, t, which], sib).wait_recv()

    def send_halo(l, t):
        @pl.when(has_right)
        def _():
            halo(l, t, 0).start()

        @pl.when(has_left)
        def _():
            halo(l, t, 1).start()

        halo(l, t, 2).start()

    def convolve(l, t):
        now = xs[2 + t]
        before = xs[1 + t - lax.rem(l, 2)]
        pre = jnp.dot(
            jnp.concatenate([before, now], axis=1), wc[l].reshape(2 * ch, 2 * ch), preferred_element_type=F32
        )
        gate = 0.5 * jnp.tanh(0.5 * pre[:, ch:]) + 0.5
        hb[l, t, 2] = (jnp.tanh(pre[:, :ch]) * gate).astype(BF16)

    @pl.when(native)
    def _():
        feat_local.wait()

    @pl.when(jnp.logical_not(native))
    def _():
        feat_copy.wait_recv()

    need(0, 0)
    for t in range(steps):
        convolve(0, t)
        send_halo(0, t)

    @pl.when(native)
    def _():
        own_local.wait()

    @pl.when(jnp.logical_not(native))
    def _():
        for step in range(YS - 1):
            plane_land(1, 0, step).wait_recv()

    swap_copy.start()

    @pl.when(outer_native)
    def _():
        outer_local.wait()

    @pl.when(both(in_valid, jnp.logical_not(outer_native)))
    def _():
        for step in range(YS - 1):
            plane_land(2 * c, 1, step).wait_recv()

    before(1 - CONV_AHEAD[2], 0)
    swap_land.wait_recv()
    for e in range(2):
        mid = rows[1, :, e].reshape(tile, 3 * tile)
        for col in range(5):
            inside = mid[:, (col - 1) * tile : col * tile] if 0 < col < 4 else jnp.zeros((tile, tile), BF16)
            hops[col, e * tile : (e + 1) * tile] = inside
        for col in range(5):
            total = jnp.zeros((tile, tile), F32)
            for via in range(3):
                if 0 <= col - via < 3:
                    total = total + jnp.dot(
                        mid[:, via * tile : (via + 1) * tile],
                        rows[via, :, e, :, (col - via) * tile : (col - via + 1) * tile].reshape(tile, tile),
                        preferred_element_type=F32,
                    )
            hops[col, (2 + e) * tile : (3 + e) * tile] = total.astype(BF16)
    for i in range(4):
        near_hops[:, i * tile : (i + 1) * tile] = hops[c + i]
    far_hops[...] = hops[4 - 4 * c, 2 * tile :]

    def hand_on(l, t):
        @pl.when(outer_ok)
        def _():
            landed(l, t, 1 + 2 * c, 1 - c)
            halo(l, t, 3).start()
            landed(l, t, 4 * c, c)

    def out_copy(section, t):
        return remote(
            obuf.at[t, section],
            out.at[m, t],
            out_send.at[section, t],
            out_recv.at[m, t],
            device(section, r),
        )

    def out_local(section, t, sample):
        return pltpu.make_async_copy(obuf.at[t, section], out.at[sample, t], out_recv.at[sample, t])

    def finish(t):
        if t == 0:
            need(last_layer, 1)
        result = tot[t * tile : (t + 1) * tile] + jnp.dot(
            hb[last_layer, t, 2], wm[last_layer, 0:4].reshape(ch, ch), preferred_element_type=F32
        )
        obuf[t] = result.astype(BF16).reshape(layers, tile // layers, ch)
        for section in range(layers):
            keep = both(at_home, s == section)

            @pl.when(keep)
            def _():
                out_local(section, t, m).start()

            @pl.when(jnp.logical_not(keep))
            def _():
                out_copy(section, t).start()

    @pl.loop(0, last_layer)
    def _(l):
        need(l, 1)
        own = hb[l, :, 2].reshape(steps * tile, ch)
        tot[...] += jnp.dot(own, wm[l, 0:4].reshape(ch, ch), preferred_element_type=F32)
        base[...] = xs[2:].reshape(steps * tile, ch).astype(F32) + jnp.dot(
            own, wm[l, 4:8].reshape(ch, ch), preferred_element_type=F32
        )
        hand_on(l, 0)
        for t in range(steps):
            landed(l, t, 3 - 2 * c, 2)
            fields = jnp.dot(
                near_hops[...], hb[l, t, pl.ds(c, 4)].reshape(4 * tile, ch), preferred_element_type=F32
            ).astype(BF16)
            wide = jnp.concatenate([fields[i * tile : (i + 1) * tile] for i in range(4)], axis=1)
            mixed = base[t * tile : (t + 1) * tile] + jnp.dot(
                wide, wm[l, 8:24].reshape(4 * ch, ch), preferred_element_type=F32
            )
            if t < steps - 1:
                hand_on(l, t + 1)
            point(l, t)

            @pl.when(inner_ok)
            def _():
                landed(l, t, 4 - 4 * c, 3)

            fields = jnp.dot(far_hops[...], hb[l, t, 4 - 4 * c], preferred_element_type=F32).astype(BF16)
            wide = jnp.concatenate([fields[:tile], fields[tile:]], axis=1)
            mixed = mixed + jnp.dot(wide, wm[l, 16:24].reshape(2 * ch, ch), preferred_element_type=F32)
            xs[2 + t] = mixed.astype(BF16)
            if t == 0:
                need(l + 1, 0)
            convolve(l + 1, t)

            @pl.when(l < last_layer - 1)
            def _():
                send_halo(l + 1, t)

            @pl.when(l == last_layer - 1)
            def _():
                finish(t)

    @pl.when(jnp.logical_not(native))
    def _():
        feat_copy.wait_send()
        own_copy.wait_send()
        for step in range(YS - 1):
            plane_copy(1, 0, step).wait_send()

    @pl.when(both(out_valid, jnp.logical_not(outer_native)))
    def _():
        outer_copy.wait_send()

    @pl.when(both(in_valid, jnp.logical_not(outer_native)))
    def _():
        for step in range(YS - 1):
            plane_copy(2 * c, 1, step).wait_send()

    swap_copy.wait_send()

    @pl.loop(0, last_layer)
    def _(l):
        for t in range(steps):
            @pl.when(has_right)
            def _():
                halo(l, t, 0).wait_send()

            @pl.when(has_left)
            def _():
                halo(l, t, 1).wait_send()

            halo(l, t, 2).wait_send()

            @pl.when(outer_ok)
            def _():
                halo(l, t, 3).wait_send()

        drain_weights(l)

    drain_weights(last_layer)

    for section in range(layers):
        @pl.when(jnp.logical_not(both(at_home, s == section)))
        def _():
            for t in range(steps):
                out_copy(section, t).wait_send()

    for sample in range(layers):
        keep = both(at_home, m == sample)

        @pl.when(keep)
        def _():
            for t in range(steps):
                out_local(s, t, sample).wait()

        @pl.when(jnp.logical_not(keep))
        def _():
            for t in range(steps):
                ref = out.at[sample, t]
                remote(obuf.at[t, 0], ref, out_send.at[sample, t], out_recv.at[sample, t], sib).wait_recv()


def body(
    features_in,
    filter_gate,
    self_mix,
    hop_one_mix,
    hop_two_mix,
    skip_weight,
    tile_values,
    tile_columns,
    tile_counts,
):
    micro, tile, steps, ch = features_in.shape
    layers = lax.axis_size("section")
    blocks = lax.axis_size("node")
    part = ch // 4
    feat = features_in.transpose(0, 2, 1, 3)
    dma = pltpu.SemaphoreType.DMA
    in_hbm = pl.BlockSpec(memory_space=pltpu.HBM)
    in_vmem = pl.BlockSpec(memory_space=pltpu.VMEM)
    in_smem = pl.BlockSpec(memory_space=pltpu.SMEM)
    landed = pl.pallas_call(
        functools.partial(kernel, layers, blocks),
        out_shape=jax.ShapeDtypeStruct((micro, steps, tile // layers, ch), BF16),
        in_specs=[in_hbm] * 6 + [in_vmem, in_smem, in_smem],
        out_specs=in_hbm,
        scratch_shapes=[
            pltpu.VMEM((2 + steps, tile, ch), BF16),
            pltpu.VMEM((layers, steps, 5, tile, ch), BF16),
            pltpu.VMEM((layers, 8, ch // 4, 2 * ch), BF16),
            pltpu.VMEM((layers, 24, part, ch), BF16),
            pltpu.VMEM((YS, 2, tile // YS, 3 * tile), BF16),
            pltpu.VMEM((3, YS, 2, tile // YS, 3 * tile), BF16),
            pltpu.VMEM((5, 4 * tile, tile), BF16),
            pltpu.VMEM((4 * tile, 4 * tile), BF16),
            pltpu.VMEM((2 * tile, tile), BF16),
            pltpu.VMEM((steps * tile, ch), F32),
            pltpu.VMEM((steps * tile, ch), F32),
            pltpu.VMEM((steps, layers, tile // layers, ch), BF16),
            dma((5,)),
            dma((2,)),
            dma((3,)),
            dma((3,)),
            dma((2, 3)),
            dma((2, 3)),
            dma((layers - 1, steps, 4)),
            dma((layers - 1, steps, 4)),
            dma((layers, 2, 7)),
            dma((layers, 2)),
            dma((layers, 2, 3)),
            dma((layers, 2)),
            dma((layers, steps)),
            dma((layers, steps)),
        ],
        compiler_params=pltpu.CompilerParams(
            collective_id=0, has_side_effects=True, vmem_limit_bytes=62 * 1024 * 1024
        ),
        cost_estimate=pl.CostEstimate(flops=7_000_000_000, bytes_accessed=4_000_000, transcendentals=3_000_000),
    )(
        feat,
        filter_gate.reshape(8, ch // 4, 2 * ch),
        self_mix.reshape(4, part, ch),
        hop_one_mix.reshape(8, part, ch),
        hop_two_mix.reshape(8, part, ch),
        skip_weight.reshape(4, part, ch),
        tile_values[:, 0],
        tile_columns[:, 0],
        tile_counts,
    )
    return landed.transpose(0, 2, 1, 3).astype(F32)[:, None]


def solution(mesh):
    in_specs = (
        P(None, "node", None, None),
        P("section", None, None, None),
        P("section", None, None),
        P("section", None, None, None),
        P("section", None, None, None),
        P("section", None, None),
        P(None, "node", None, None, None),
        P(None, "node", None),
        P(None, "node"),
    )
    out_specs = P(None, "node", "section", None, None)
    return jax.shard_map(body, mesh=mesh, in_specs=in_specs, out_specs=out_specs, check_vma=False)
```

```python
import functools

import jax
import jax.numpy as jnp
from jax import lax
from jax.experimental import pallas as pl
from jax.experimental.pallas import tpu as pltpu
from jax.sharding import PartitionSpec as P

F32 = jnp.float32
BF16 = jnp.bfloat16
MESH = pl.DeviceIdType.MESH
XS = 4
YS = 4
CONV_AHEAD = (15, 10, 4)
MIX_AHEAD = (15, 9, 3)
START = max(CONV_AHEAD + MIX_AHEAD)
SHARED = 8


def both(*conds):
    out = conds[0]
    for cond in conds[1:]:
        out = jnp.logical_and(out, cond)
    return out


def kernel(
    layers,
    blocks,
    feat,
    conv_in,
    self_in,
    one_in,
    two_in,
    skip_in,
    tiles,
    columns,
    counts,
    out,
    xs,
    hb,
    wc,
    wm,
    near,
    rows,
    hops,
    near_hops,
    far_hops,
    base,
    tot,
    obuf,
    load_sem,
    feat_sem,
    tile_send,
    tile_recv,
    plane_send,
    plane_recv,
    halo_send,
    halo_recv,
    w_send,
    w_recv,
    w_quad,
    w_sib,
    out_send,
    out_recv,
):
    _, steps, tile, ch = feat.shape
    last_layer = layers - 1
    s = lax.axis_index("section")
    n = lax.axis_index("node")
    y, c = lax.div(s, 2), lax.rem(s, 2)
    z, x = lax.div(n, XS), lax.rem(n, XS)
    last = blocks // 2 - 1

    group = lax.rem(lax.div(x + 1, 2), 2)
    side = lax.div(x, 2)
    place = side + lax.rem(z, 2) * (1 - 2 * side)
    k = 2 * z + place
    r = 2 * k + c
    m = 2 * y + group

    def node_at(group, k):
        z, place = lax.div(k, 2), lax.rem(k, 2)
        side = place + lax.rem(z, 2) * (1 - 2 * place)
        return XS * z + group + side * (3 - 2 * group)

    def device(section, node):
        return {"section": section, "node": node}

    def worker(sample, block):
        return device(
            2 * lax.div(sample, 2) + lax.rem(block, 2), node_at(lax.rem(sample, 2), lax.div(block, 2))
        )

    def remote(src, dst, send, recv, dev):
        return pltpu.make_async_remote_copy(
            src_ref=src, dst_ref=dst, send_sem=send, recv_sem=recv, device_id=dev, device_id_type=MESH
        )

    sib = device(2 * y + 1 - c, n)
    right = device(2 * y, node_at(group, jnp.minimum(k + 1, last)))
    left = device(2 * y + 1, node_at(group, jnp.maximum(k - 1, 0)))
    has_right, has_left = k < last, k > 0
    outer_ok = jnp.where(c == 0, has_left, has_right)
    inner_ok = jnp.where(c == 0, has_right, has_left)
    outer_k = jnp.clip(k - 1 + 2 * c, 0, last)

    zs = blocks // XS
    odd_x = lax.rem(x, 2)
    low_z = lax.rem(z + side, 2)
    quad = odd_x + 2 * low_z
    quad_x = x + 1 - 2 * odd_x
    quad_z = lax.rem(z + 1 - 2 * low_z + zs, zs)
    quad_devices = [device(s, XS * z + quad_x), device(s, XS * quad_z + x), device(s, XS * quad_z + quad_x)]
    flip_x, flip_z = 1 - 2 * odd_x, 2 - 4 * low_z
    quad_parts = [quad + flip_x, quad + flip_z, quad + flip_x + flip_z]

    at_home = n == r
    native = both(s == m, at_home)
    mine_to = worker(s, n)
    mine_from = device(m, r)
    n_out = n + 2 * lax.rem(n, 2) - 1
    r_out = r - 1 + 2 * c
    out_slot = 2 * (1 - lax.rem(n, 2))
    out_valid = both(n_out >= 0, n_out < blocks)
    in_valid = both(r_out >= 0, r_out < blocks)
    outer_to = worker(s, jnp.clip(n_out, 0, blocks - 1))
    outer_from = device(m, jnp.clip(r_out, 0, blocks - 1))
    outer_native = both(s == m, n == r_out)

    loads = [
        pltpu.make_async_copy(conv_in, wc.at[s], load_sem.at[0]),
        pltpu.make_async_copy(skip_in, wm.at[s, pl.ds(0, 4)], load_sem.at[1]),
        pltpu.make_async_copy(self_in, wm.at[s, pl.ds(4, 4)], load_sem.at[2]),
        pltpu.make_async_copy(one_in, wm.at[s, pl.ds(8, 8)], load_sem.at[3]),
        pltpu.make_async_copy(two_in, wm.at[s, pl.ds(16, 8)], load_sem.at[4]),
    ]
    for load in loads:
        load.start()

    barrier = pltpu.get_barrier_semaphore()

    def greet(dev):
        pl.semaphore_signal(barrier, inc=1, device_id=dev, device_id_type=MESH)

    greet(sib)
    for friend in quad_devices:
        greet(friend)
    for step in range(1, YS):
        for core in range(2):
            greet(device(2 * lax.rem(y + step, YS) + core, n))

    @pl.when(outer_ok)
    def _():
        for core in range(2):
            greet(device(2 * y + core, node_at(group, outer_k)))

    @pl.when(jnp.logical_not(native))
    def _():
        greet(mine_from)

    @pl.when(both(in_valid, jnp.logical_not(outer_native)))
    def _():
        greet(outer_from)

    for sample in range(layers):
        @pl.when(jnp.logical_not(both(at_home, m == sample)))
        def _():
            greet(worker(sample, n))

    for e in range(2):
        for w in range(3):
            total = jnp.zeros((tile, tile), F32)
            for slot in range(3):
                weight = both(columns[e, slot] == n - 1 + w, slot < counts[e, 0]).astype(F32)
                total = total + tiles[e, slot].astype(F32) * weight
            near[:, e, :, w * tile : (w + 1) * tile] = total.astype(BF16).reshape(YS, tile // YS, tile)
    xs[0:2] = jnp.zeros((2, tile, ch), BF16)
    tot[...] = jnp.zeros_like(tot)

    @pl.when(jnp.logical_not(outer_ok))
    def _():
        rows[2 * c] = jnp.zeros(near.shape, BF16)

        @pl.loop(0, last_layer)
        def _(layer):
            for t in range(steps):
                hb[layer, t, 3 * c] = jnp.zeros((tile, ch), BF16)
                hb[layer, t, 3 * c + 1] = jnp.zeros((tile, ch), BF16)

    @pl.when(jnp.logical_not(inner_ok))
    def _():
        @pl.loop(0, last_layer)
        def _(layer):
            for t in range(steps):
                hb[layer, t, 4 - 4 * c] = jnp.zeros((tile, ch), BF16)

    as_int = lambda cond: cond.astype(jnp.int32)
    expected = (
        1
        + 3
        + 2 * (YS - 1)
        + as_int(has_right)
        + as_int(has_left)
        + 1
        - as_int(native)
        + as_int(both(out_valid, jnp.logical_not(outer_native)))
        + layers
        - as_int(at_home)
    )
    pl.semaphore_wait(barrier, expected)
    for load in loads:
        load.wait()

    def piece(layer, kind, first, count):
        return wc.at[layer, pl.ds(first, count)] if kind == 0 else wm.at[layer, pl.ds(3 * first, 3 * count)]

    others = [lax.rem(y + step, YS) for step in range(1, YS)]

    def owner_copy(layer, kind, step, core, shared):
        ref = piece(layer, kind, 4 * core + quad, 1) if shared else piece(layer, kind, 4 * core, 4)
        return remote(
            ref,
            ref,
            w_send.at[layer, kind, 2 * step + core],
            w_recv.at[layer, kind],
            device(2 * others[step] + core, n),
        )

    def owner_land(layer, kind, shared):
        ref = piece(layer, kind, 4 * c + quad, 1) if shared else piece(layer, kind, 4 * c, 4)
        return remote(ref, ref, w_send.at[layer, kind, 0], w_recv.at[layer, kind], sib)

    def quad_copy(layer, kind, i):
        ref = piece(layer, kind, 4 * c + quad, 1)
        return remote(ref, ref, w_send.at[layer, kind, i], w_quad.at[layer, kind, i], quad_devices[i])

    def quad_land(layer, kind, i):
        ref = piece(layer, kind, 4 * c + quad_parts[i], 1)
        return remote(ref, ref, w_send.at[layer, kind, i], w_quad.at[layer, kind, i], sib)

    def whole_copy(layer, kind):
        ref = piece(layer, kind, 0, 8)
        return remote(ref, ref, w_send.at[layer, kind, 6], w_sib.at[layer, kind], sib)

    def half_copy(layer, kind, core):
        ref = piece(layer, kind, 4 * core, 4)
        return remote(ref, ref, w_send.at[layer, kind, 6], w_sib.at[layer, kind], sib)

    def deal(layer, kind, stage, valid):
        same = lax.div(layer, 2) == y
        apart = both(valid, jnp.logical_not(same))
        early = layer < SHARED
        late = jnp.logical_not(early)
        if stage == 0:
            mine = both(valid, same, lax.rem(layer, 2) == c)
            for shared, when in ((True, early), (False, late)):
                @pl.when(both(mine, when))
                def _():
                    for step in (1, 0, 2):
                        for core in range(2):
                            owner_copy(layer, kind, step, core, shared).start()

            @pl.when(mine)
            def _():
                whole_copy(layer, kind).start()
        elif stage == 1:
            @pl.when(both(apart, early))
            def _():
                owner_land(layer, kind, True).wait_recv()
                for i in (2, 0, 1):
                    quad_copy(layer, kind, i).start()

            @pl.when(both(apart, late))
            def _():
                owner_land(layer, kind, False).wait_recv()
                half_copy(layer, kind, c).start()
        else:
            @pl.when(both(apart, early))
            def _():
                for i in range(3):
                    quad_land(layer, kind, i).wait_recv()
                half_copy(layer, kind, c).start()

    events = [
        (kind, stage, ahead) for kind, table in ((0, CONV_AHEAD), (1, MIX_AHEAD)) for stage, ahead in enumerate(table)
    ]
    events.sort(key=lambda event: (event[1] > 0, event[2]))

    def point(l, t):
        for kind, stage, ahead in events:
            if (t + ahead) % 3 == 0:
                layer = l + (t + ahead) // 3
                deal(jnp.minimum(layer, last_layer), kind, stage, layer <= last_layer)

    def before(first, stop):
        for step in range(first, stop):
            for kind, stage, ahead in events:
                if (step + ahead) % 3 == 0 and 0 <= step + ahead < 3 * layers:
                    deal(jnp.int32((step + ahead) // 3), kind, stage, jnp.bool_(True))

    def need(layer, kind):
        same = lax.div(layer, 2) == y

        @pl.when(jnp.logical_not(same))
        def _():
            half_copy(layer, kind, 1 - c).wait_recv()

        @pl.when(both(same, lax.rem(layer, 2) != c))
        def _():
            whole_copy(layer, kind).wait_recv()

    def drain_weights(layer):
        same = lax.div(layer, 2) == y
        early = layer < SHARED
        for kind in range(2):
            for shared, when in ((True, early), (False, jnp.logical_not(early))):
                @pl.when(both(same, lax.rem(layer, 2) == c, when))
                def _():
                    for step in range(YS - 1):
                        for core in range(2):
                            owner_copy(layer, kind, step, core, shared).wait_send()

            @pl.when(both(same, lax.rem(layer, 2) == c))
            def _():
                whole_copy(layer, kind).wait_send()

            @pl.when(both(jnp.logical_not(same), early))
            def _():
                for i in range(3):
                    quad_copy(layer, kind, i).wait_send()

            @pl.when(jnp.logical_not(same))
            def _():
                half_copy(layer, kind, c).wait_send()

    mine = feat.at[s]
    feat_copy = remote(mine, xs.at[pl.ds(2, steps)], feat_sem.at[0], feat_sem.at[1], mine_to)
    feat_local = pltpu.make_async_copy(mine, xs.at[pl.ds(2, steps)], feat_sem.at[1])
    own_copy = remote(near.at[y], rows.at[1, y], tile_send.at[0], tile_recv.at[0], mine_to)
    own_local = pltpu.make_async_copy(near, rows.at[1], tile_recv.at[0])
    outer_copy = remote(near.at[y], rows.at[out_slot, y], tile_send.at[1], tile_recv.at[1], outer_to)
    outer_local = pltpu.make_async_copy(near, rows.at[2 * c], tile_recv.at[1])
    outer_land = remote(near.at[y], rows.at[2 * c, y], tile_send.at[1], tile_recv.at[1], outer_to)
    swap_copy = remote(rows.at[1], rows.at[2 * c], tile_send.at[2], tile_recv.at[2], sib)
    def plane_copy(slot, which, step):
        ref = rows.at[slot, y]
        return remote(
            ref, ref, plane_send.at[which, step], plane_recv.at[which, step], device(2 * others[step] + c, n)
        )

    def plane_land(slot, which, step):
        ref = rows.at[slot, others[YS - 2 - step]]
        return remote(ref, ref, plane_send.at[which, step], plane_recv.at[which, step], sib)

    swap_land = remote(rows.at[1], rows.at[2 - 2 * c], tile_send.at[2], tile_recv.at[2], sib)

    before(-START, 1 - CONV_AHEAD[0])

    @pl.when(native)
    def _():
        feat_local.start()
        own_local.start()

    @pl.when(jnp.logical_not(native))
    def _():
        feat_copy.start()
        own_copy.start()

    @pl.when(outer_native)
    def _():
        outer_local.start()

    @pl.when(both(out_valid, jnp.logical_not(outer_native)))
    def _():
        outer_copy.start()

    before(1 - CONV_AHEAD[0], 1 - CONV_AHEAD[1])

    @pl.when(jnp.logical_not(native))
    def _():
        own_copy.wait_recv()
        for step in range(YS - 1):
            plane_copy(1, 0, step).start()

    @pl.when(both(in_valid, jnp.logical_not(outer_native)))
    def _():
        outer_land.wait_recv()
        for step in range(YS - 1):
            plane_copy(2 * c, 1, step).start()

    before(1 - CONV_AHEAD[1], 1 - CONV_AHEAD[2])

    def halo(l, t, which):
        own = hb.at[l, t, 2]
        if which == 0:
            return remote(own, hb.at[l, t, c], halo_send.at[l, t, 0], halo_recv.at[l, t, c], right)
        if which == 1:
            return remote(own, hb.at[l, t, c + 3], halo_send.at[l, t, 1], halo_recv.at[l, t, c], left)
        if which == 2:
            return remote(own, hb.at[l, t, 1 + 2 * c], halo_send.at[l, t, 2], halo_recv.at[l, t, 2], sib)
        return remote(
            hb.at[l, t, 1 + 2 * c], hb.at[l, t, 4 * c], halo_send.at[l, t, 3], halo_recv.at[l, t, 3], sib
        )

    def landed(l, t, slot, which):
        ref = hb.at[l, t, slot]
        remote(ref, ref, halo_send.at[l, t, 3], halo_recv.at[l, t, which], sib).wait_recv()

    def send_halo(l, t):
        @pl.when(both(has_right, c == 1))
        def _():
            halo(l, t, 0).start()

        @pl.when(has_left)
        def _():
            halo(l, t, 1).start()

        @pl.when(both(has_right, c == 0))
        def _():
            halo(l, t, 0).start()

        halo(l, t, 2).start()

    def convolve(l, t):
        now = xs[2 + t]
        before = xs[1 + t - lax.rem(l, 2)]
        pre = jnp.dot(
            jnp.concatenate([before, now], axis=1), wc[l].reshape(2 * ch, 2 * ch), preferred_element_type=F32
        )
        gate = 0.5 * jnp.tanh(0.5 * pre[:, ch:]) + 0.5
        hb[l, t, 2] = (jnp.tanh(pre[:, :ch]) * gate).astype(BF16)

    @pl.when(native)
    def _():
        feat_local.wait()

    @pl.when(jnp.logical_not(native))
    def _():
        feat_copy.wait_recv()

    need(0, 0)
    for t in range(steps):
        convolve(0, t)
        send_halo(0, t)

    @pl.when(native)
    def _():
        own_local.wait()

    @pl.when(jnp.logical_not(native))
    def _():
        for step in range(YS - 1):
            plane_land(1, 0, step).wait_recv()

    swap_copy.start()

    @pl.when(outer_native)
    def _():
        outer_local.wait()

    @pl.when(both(in_valid, jnp.logical_not(outer_native)))
    def _():
        for step in range(YS - 1):
            plane_land(2 * c, 1, step).wait_recv()

    before(1 - CONV_AHEAD[2], 0)
    swap_land.wait_recv()
    for e in range(2):
        mid = rows[1, :, e].reshape(tile, 3 * tile)
        for col in range(5):
            inside = mid[:, (col - 1) * tile : col * tile] if 0 < col < 4 else jnp.zeros((tile, tile), BF16)
            hops[col, e * tile : (e + 1) * tile] = inside
        for col in range(5):
            total = jnp.zeros((tile, tile), F32)
            for via in range(3):
                if 0 <= col - via < 3:
                    total = total + jnp.dot(
                        mid[:, via * tile : (via + 1) * tile],
                        rows[via, :, e, :, (col - via) * tile : (col - via + 1) * tile].reshape(tile, tile),
                        preferred_element_type=F32,
                    )
            hops[col, (2 + e) * tile : (3 + e) * tile] = total.astype(BF16)
    for i in range(4):
        near_hops[:, i * tile : (i + 1) * tile] = hops[c + i]
    far_hops[...] = hops[4 - 4 * c, 2 * tile :]

    def hand_on(l, t):
        @pl.when(outer_ok)
        def _():
            landed(l, t, 1 + 2 * c, 1 - c)
            halo(l, t, 3).start()

    def out_copy(section, t):
        return remote(
            obuf.at[t, section],
            out.at[m, t],
            out_send.at[section, t],
            out_recv.at[m, t],
            device(section, r),
        )

    def out_local(section, t, sample):
        return pltpu.make_async_copy(obuf.at[t, section], out.at[sample, t], out_recv.at[sample, t])

    def finish(t):
        if t == 0:
            need(last_layer, 1)
        result = tot[t * tile : (t + 1) * tile] + jnp.dot(
            hb[last_layer, t, 2], wm[last_layer, 0:4].reshape(ch, ch), preferred_element_type=F32
        )
        obuf[t] = result.astype(BF16).reshape(layers, tile // layers, ch)
        for section in range(layers):
            keep = both(at_home, s == section)

            @pl.when(keep)
            def _():
                out_local(section, t, m).start()

            @pl.when(jnp.logical_not(keep))
            def _():
                out_copy(section, t).start()

    @pl.loop(0, last_layer)
    def _(l):
        need(l, 1)
        own = hb[l, :, 2].reshape(steps * tile, ch)
        tot[...] += jnp.dot(own, wm[l, 0:4].reshape(ch, ch), preferred_element_type=F32)
        base[...] = xs[2:].reshape(steps * tile, ch).astype(F32) + jnp.dot(
            own, wm[l, 4:8].reshape(ch, ch), preferred_element_type=F32
        )
        hand_on(l, 0)
        for t in range(steps):
            landed(l, t, 3 - 2 * c, 2)

            @pl.when(outer_ok)
            def _():
                landed(l, t, 4 * c, c)

            fields = jnp.dot(
                near_hops[...], hb[l, t, pl.ds(c, 4)].reshape(4 * tile, ch), preferred_element_type=F32
            ).astype(BF16)
            wide = jnp.concatenate([fields[i * tile : (i + 1) * tile] for i in range(4)], axis=1)
            mixed = base[t * tile : (t + 1) * tile] + jnp.dot(
                wide, wm[l, 8:24].reshape(4 * ch, ch), preferred_element_type=F32
            )
            point(l, t)

            @pl.when(inner_ok)
            def _():
                landed(l, t, 4 - 4 * c, 3)

            if t < steps - 1:
                hand_on(l, t + 1)

            fields = jnp.dot(far_hops[...], hb[l, t, 4 - 4 * c], preferred_element_type=F32).astype(BF16)
            wide = jnp.concatenate([fields[:tile], fields[tile:]], axis=1)
            mixed = mixed + jnp.dot(wide, wm[l, 16:24].reshape(2 * ch, ch), preferred_element_type=F32)
            xs[2 + t] = mixed.astype(BF16)
            if t == 0:
                need(l + 1, 0)
            convolve(l + 1, t)

            @pl.when(l < last_layer - 1)
            def _():
                send_halo(l + 1, t)

            @pl.when(l == last_layer - 1)
            def _():
                finish(t)

    @pl.when(jnp.logical_not(native))
    def _():
        feat_copy.wait_send()
        own_copy.wait_send()
        for step in range(YS - 1):
            plane_copy(1, 0, step).wait_send()

    @pl.when(both(out_valid, jnp.logical_not(outer_native)))
    def _():
        outer_copy.wait_send()

    @pl.when(both(in_valid, jnp.logical_not(outer_native)))
    def _():
        for step in range(YS - 1):
            plane_copy(2 * c, 1, step).wait_send()

    swap_copy.wait_send()

    @pl.loop(0, last_layer)
    def _(l):
        for t in range(steps):
            @pl.when(has_right)
            def _():
                halo(l, t, 0).wait_send()

            @pl.when(has_left)
            def _():
                halo(l, t, 1).wait_send()

            halo(l, t, 2).wait_send()

            @pl.when(outer_ok)
            def _():
                halo(l, t, 3).wait_send()

        drain_weights(l)

    drain_weights(last_layer)

    for section in range(layers):
        @pl.when(jnp.logical_not(both(at_home, s == section)))
        def _():
            for t in range(steps):
                out_copy(section, t).wait_send()

    for sample in range(layers):
        keep = both(at_home, m == sample)

        @pl.when(keep)
        def _():
            for t in range(steps):
                out_local(s, t, sample).wait()

        @pl.when(jnp.logical_not(keep))
        def _():
            for t in range(steps):
                ref = out.at[sample, t]
                remote(obuf.at[t, 0], ref, out_send.at[sample, t], out_recv.at[sample, t], sib).wait_recv()


def body(
    features_in,
    filter_gate,
    self_mix,
    hop_one_mix,
    hop_two_mix,
    skip_weight,
    tile_values,
    tile_columns,
    tile_counts,
):
    micro, tile, steps, ch = features_in.shape
    layers = lax.axis_size("section")
    blocks = lax.axis_size("node")
    part = ch // 4
    feat = features_in.transpose(0, 2, 1, 3)
    dma = pltpu.SemaphoreType.DMA
    in_hbm = pl.BlockSpec(memory_space=pltpu.HBM)
    in_vmem = pl.BlockSpec(memory_space=pltpu.VMEM)
    in_smem = pl.BlockSpec(memory_space=pltpu.SMEM)
    landed = pl.pallas_call(
        functools.partial(kernel, layers, blocks),
        out_shape=jax.ShapeDtypeStruct((micro, steps, tile // layers, ch), BF16),
        in_specs=[in_hbm] * 6 + [in_vmem, in_smem, in_smem],
        out_specs=in_hbm,
        scratch_shapes=[
            pltpu.VMEM((2 + steps, tile, ch), BF16),
            pltpu.VMEM((layers, steps, 5, tile, ch), BF16),
            pltpu.VMEM((layers, 8, ch // 4, 2 * ch), BF16),
            pltpu.VMEM((layers, 24, part, ch), BF16),
            pltpu.VMEM((YS, 2, tile // YS, 3 * tile), BF16),
            pltpu.VMEM((3, YS, 2, tile // YS, 3 * tile), BF16),
            pltpu.VMEM((5, 4 * tile, tile), BF16),
            pltpu.VMEM((4 * tile, 4 * tile), BF16),
            pltpu.VMEM((2 * tile, tile), BF16),
            pltpu.VMEM((steps * tile, ch), F32),
            pltpu.VMEM((steps * tile, ch), F32),
            pltpu.VMEM((steps, layers, tile // layers, ch), BF16),
            dma((5,)),
            dma((2,)),
            dma((3,)),
            dma((3,)),
            dma((2, 3)),
            dma((2, 3)),
            dma((layers - 1, steps, 4)),
            dma((layers - 1, steps, 4)),
            dma((layers, 2, 7)),
            dma((layers, 2)),
            dma((layers, 2, 3)),
            dma((layers, 2)),
            dma((layers, steps)),
            dma((layers, steps)),
        ],
        compiler_params=pltpu.CompilerParams(
            collective_id=0, has_side_effects=True, vmem_limit_bytes=62 * 1024 * 1024
        ),
        cost_estimate=pl.CostEstimate(flops=7_000_000_000, bytes_accessed=4_000_000, transcendentals=3_000_000),
    )(
        feat,
        filter_gate.reshape(8, ch // 4, 2 * ch),
        self_mix.reshape(4, part, ch),
        hop_one_mix.reshape(8, part, ch),
        hop_two_mix.reshape(8, part, ch),
        skip_weight.reshape(4, part, ch),
        tile_values[:, 0],
        tile_columns[:, 0],
        tile_counts,
    )
    return landed.transpose(0, 2, 1, 3).astype(F32)[:, None]


def solution(mesh):
    in_specs = (
        P(None, "node", None, None),
        P("section", None, None, None),
        P("section", None, None),
        P("section", None, None, None),
        P("section", None, None, None),
        P("section", None, None),
        P(None, "node", None, None, None),
        P(None, "node", None),
        P(None, "node"),
    )
    out_specs = P(None, "node", "section", None, None)
    return jax.shard_map(body, mesh=mesh, in_specs=in_specs, out_specs=out_specs, check_vma=False)
```

```python
import functools

import jax
import jax.numpy as jnp
from jax import lax
from jax.experimental import pallas as pl
from jax.experimental.pallas import tpu as pltpu
from jax.sharding import PartitionSpec as P

F32 = jnp.float32
BF16 = jnp.bfloat16
MESH = pl.DeviceIdType.MESH
XS = 4
YS = 4
CONV_AHEAD = (15, 10, 4)
MIX_AHEAD = (15, 9, 3)
START = max(CONV_AHEAD + MIX_AHEAD)
SHARED = 8


def both(*conds):
    out = conds[0]
    for cond in conds[1:]:
        out = jnp.logical_and(out, cond)
    return out


def kernel(
    layers,
    blocks,
    feat,
    conv_in,
    self_in,
    one_in,
    two_in,
    skip_in,
    tiles,
    columns,
    counts,
    out,
    xs,
    hb,
    wc,
    wm,
    near,
    rows,
    hops,
    near_hops,
    far_hops,
    base,
    tot,
    obuf,
    load_sem,
    feat_sem,
    tile_send,
    tile_recv,
    plane_send,
    plane_recv,
    halo_send,
    halo_recv,
    w_send,
    w_recv,
    w_quad,
    w_sib,
    out_send,
    out_recv,
):
    _, steps, tile, ch = feat.shape
    last_layer = layers - 1
    s = lax.axis_index("section")
    n = lax.axis_index("node")
    y, c = lax.div(s, 2), lax.rem(s, 2)
    z, x = lax.div(n, XS), lax.rem(n, XS)
    last = blocks // 2 - 1

    group = lax.rem(lax.div(x + 1, 2), 2)
    side = lax.div(x, 2)
    place = side + lax.rem(z, 2) * (1 - 2 * side)
    k = 2 * z + place
    r = 2 * k + c
    m = 2 * y + group

    def node_at(group, k):
        z, place = lax.div(k, 2), lax.rem(k, 2)
        side = place + lax.rem(z, 2) * (1 - 2 * place)
        return XS * z + group + side * (3 - 2 * group)

    def device(section, node):
        return {"section": section, "node": node}

    def worker(sample, block):
        return device(
            2 * lax.div(sample, 2) + lax.rem(block, 2), node_at(lax.rem(sample, 2), lax.div(block, 2))
        )

    def remote(src, dst, send, recv, dev):
        return pltpu.make_async_remote_copy(
            src_ref=src, dst_ref=dst, send_sem=send, recv_sem=recv, device_id=dev, device_id_type=MESH
        )

    sib = device(2 * y + 1 - c, n)
    right = device(2 * y, node_at(group, jnp.minimum(k + 1, last)))
    left = device(2 * y + 1, node_at(group, jnp.maximum(k - 1, 0)))
    has_right, has_left = k < last, k > 0
    outer_ok = jnp.where(c == 0, has_left, has_right)
    inner_ok = jnp.where(c == 0, has_right, has_left)
    outer_k = jnp.clip(k - 1 + 2 * c, 0, last)

    zs = blocks // XS
    odd_x = lax.rem(x, 2)
    low_z = lax.rem(z + side, 2)
    quad = odd_x + 2 * low_z
    quad_x = x + 1 - 2 * odd_x
    quad_z = lax.rem(z + 1 - 2 * low_z + zs, zs)
    quad_devices = [device(s, XS * z + quad_x), device(s, XS * quad_z + x), device(s, XS * quad_z + quad_x)]
    flip_x, flip_z = 1 - 2 * odd_x, 2 - 4 * low_z
    quad_parts = [quad + flip_x, quad + flip_z, quad + flip_x + flip_z]

    at_home = n == r
    native = both(s == m, at_home)
    mine_to = worker(s, n)
    mine_from = device(m, r)
    n_out = n + 2 * lax.rem(n, 2) - 1
    r_out = r - 1 + 2 * c
    out_slot = 2 * (1 - lax.rem(n, 2))
    out_valid = both(n_out >= 0, n_out < blocks)
    in_valid = both(r_out >= 0, r_out < blocks)
    outer_to = worker(s, jnp.clip(n_out, 0, blocks - 1))
    outer_from = device(m, jnp.clip(r_out, 0, blocks - 1))
    outer_native = both(s == m, n == r_out)

    loads = [
        pltpu.make_async_copy(conv_in, wc.at[s], load_sem.at[0]),
        pltpu.make_async_copy(skip_in, wm.at[s, pl.ds(0, 4)], load_sem.at[1]),
        pltpu.make_async_copy(self_in, wm.at[s, pl.ds(4, 4)], load_sem.at[2]),
        pltpu.make_async_copy(one_in, wm.at[s, pl.ds(8, 8)], load_sem.at[3]),
        pltpu.make_async_copy(two_in, wm.at[s, pl.ds(16, 8)], load_sem.at[4]),
    ]
    for load in loads:
        load.start()

    barrier = pltpu.get_barrier_semaphore()

    def greet(dev):
        pl.semaphore_signal(barrier, inc=1, device_id=dev, device_id_type=MESH)

    greet(sib)
    for friend in quad_devices:
        greet(friend)
    for step in range(1, YS):
        for core in range(2):
            greet(device(2 * lax.rem(y + step, YS) + core, n))

    @pl.when(outer_ok)
    def _():
        for core in range(2):
            greet(device(2 * y + core, node_at(group, outer_k)))

    @pl.when(jnp.logical_not(native))
    def _():
        greet(mine_from)

    @pl.when(both(in_valid, jnp.logical_not(outer_native)))
    def _():
        greet(outer_from)

    for sample in range(layers):
        @pl.when(jnp.logical_not(both(at_home, m == sample)))
        def _():
            greet(worker(sample, n))

    for e in range(2):
        for w in range(3):
            total = jnp.zeros((tile, tile), F32)
            for slot in range(3):
                weight = both(columns[e, slot] == n - 1 + w, slot < counts[e]).astype(F32)
                total = total + tiles[e, slot].astype(F32) * weight
            near[:, e, :, w * tile : (w + 1) * tile] = total.astype(BF16).reshape(YS, tile // YS, tile)
    xs[0:2] = jnp.zeros((2, tile, ch), BF16)
    tot[...] = jnp.zeros_like(tot)

    @pl.when(jnp.logical_not(outer_ok))
    def _():
        rows[2 * c] = jnp.zeros(near.shape, BF16)

        @pl.loop(0, last_layer)
        def _(layer):
            for t in range(steps):
                hb[layer, t, 3 * c] = jnp.zeros((tile, ch), BF16)
                hb[layer, t, 3 * c + 1] = jnp.zeros((tile, ch), BF16)

    @pl.when(jnp.logical_not(inner_ok))
    def _():
        @pl.loop(0, last_layer)
        def _(layer):
            for t in range(steps):
                hb[layer, t, 4 - 4 * c] = jnp.zeros((tile, ch), BF16)

    as_int = lambda cond: cond.astype(jnp.int32)
    expected = (
        1
        + 3
        + 2 * (YS - 1)
        + as_int(has_right)
        + as_int(has_left)
        + 1
        - as_int(native)
        + as_int(both(out_valid, jnp.logical_not(outer_native)))
        + layers
        - as_int(at_home)
    )
    pl.semaphore_wait(barrier, expected)
    for load in loads:
        load.wait()

    def piece(layer, kind, first, count):
        return wc.at[layer, pl.ds(first, count)] if kind == 0 else wm.at[layer, pl.ds(3 * first, 3 * count)]

    others = [lax.rem(y + step, YS) for step in range(1, YS)]

    def owner_copy(layer, kind, step, core, shared):
        ref = piece(layer, kind, 4 * core + quad, 1) if shared else piece(layer, kind, 4 * core, 4)
        return remote(
            ref,
            ref,
            w_send.at[layer, kind, 2 * step + core],
            w_recv.at[layer, kind],
            device(2 * others[step] + core, n),
        )

    def owner_land(layer, kind, shared):
        ref = piece(layer, kind, 4 * c + quad, 1) if shared else piece(layer, kind, 4 * c, 4)
        return remote(ref, ref, w_send.at[layer, kind, 0], w_recv.at[layer, kind], sib)

    def quad_copy(layer, kind, i):
        ref = piece(layer, kind, 4 * c + quad, 1)
        return remote(ref, ref, w_send.at[layer, kind, i], w_quad.at[layer, kind, i], quad_devices[i])

    def quad_land(layer, kind, i):
        ref = piece(layer, kind, 4 * c + quad_parts[i], 1)
        return remote(ref, ref, w_send.at[layer, kind, i], w_quad.at[layer, kind, i], sib)

    def whole_copy(layer, kind):
        ref = piece(layer, kind, 0, 8)
        return remote(ref, ref, w_send.at[layer, kind, 6], w_sib.at[layer, kind], sib)

    def half_copy(layer, kind, core):
        ref = piece(layer, kind, 4 * core, 4)
        return remote(ref, ref, w_send.at[layer, kind, 6], w_sib.at[layer, kind], sib)

    def deal(layer, kind, stage, valid):
        same = lax.div(layer, 2) == y
        apart = both(valid, jnp.logical_not(same))
        early = layer < SHARED
        late = jnp.logical_not(early)
        if stage == 0:
            mine = both(valid, same, lax.rem(layer, 2) == c)
            for shared, when in ((True, early), (False, late)):
                @pl.when(both(mine, when))
                def _():
                    for step in (1, 0, 2):
                        for core in range(2):
                            owner_copy(layer, kind, step, core, shared).start()

            @pl.when(mine)
            def _():
                whole_copy(layer, kind).start()
        elif stage == 1:
            @pl.when(both(apart, early))
            def _():
                owner_land(layer, kind, True).wait_recv()
                for i in (2, 0, 1):
                    quad_copy(layer, kind, i).start()

            @pl.when(both(apart, late))
            def _():
                owner_land(layer, kind, False).wait_recv()
                half_copy(layer, kind, c).start()
        else:
            @pl.when(both(apart, early))
            def _():
                for i in range(3):
                    quad_land(layer, kind, i).wait_recv()
                half_copy(layer, kind, c).start()

    events = [
        (kind, stage, ahead) for kind, table in ((0, CONV_AHEAD), (1, MIX_AHEAD)) for stage, ahead in enumerate(table)
    ]
    events.sort(key=lambda event: (event[1] > 0, event[2]))

    def point(l, t):
        for kind, stage, ahead in events:
            if (t + ahead) % 3 == 0:
                layer = l + (t + ahead) // 3
                deal(jnp.minimum(layer, last_layer), kind, stage, layer <= last_layer)

    def before(first, stop):
        for step in range(first, stop):
            for kind, stage, ahead in events:
                if (step + ahead) % 3 == 0 and 0 <= step + ahead < 3 * layers:
                    deal(jnp.int32((step + ahead) // 3), kind, stage, jnp.bool_(True))

    def need(layer, kind):
        same = lax.div(layer, 2) == y

        @pl.when(jnp.logical_not(same))
        def _():
            half_copy(layer, kind, 1 - c).wait_recv()

        @pl.when(both(same, lax.rem(layer, 2) != c))
        def _():
            whole_copy(layer, kind).wait_recv()

    def drain_weights(layer):
        same = lax.div(layer, 2) == y
        early = layer < SHARED
        for kind in range(2):
            for shared, when in ((True, early), (False, jnp.logical_not(early))):
                @pl.when(both(same, lax.rem(layer, 2) == c, when))
                def _():
                    for step in range(YS - 1):
                        for core in range(2):
                            owner_copy(layer, kind, step, core, shared).wait_send()

            @pl.when(both(same, lax.rem(layer, 2) == c))
            def _():
                whole_copy(layer, kind).wait_send()

            @pl.when(both(jnp.logical_not(same), early))
            def _():
                for i in range(3):
                    quad_copy(layer, kind, i).wait_send()

            @pl.when(jnp.logical_not(same))
            def _():
                half_copy(layer, kind, c).wait_send()

    mine = feat.at[s]
    feat_copy = remote(mine, xs.at[pl.ds(2, steps)], feat_sem.at[0], feat_sem.at[1], mine_to)
    feat_local = pltpu.make_async_copy(mine, xs.at[pl.ds(2, steps)], feat_sem.at[1])
    own_copy = remote(near.at[y], rows.at[1, y], tile_send.at[0], tile_recv.at[0], mine_to)
    own_local = pltpu.make_async_copy(near, rows.at[1], tile_recv.at[0])
    outer_copy = remote(near.at[y], rows.at[out_slot, y], tile_send.at[1], tile_recv.at[1], outer_to)
    outer_local = pltpu.make_async_copy(near, rows.at[2 * c], tile_recv.at[1])
    outer_land = remote(near.at[y], rows.at[2 * c, y], tile_send.at[1], tile_recv.at[1], outer_to)
    swap_copy = remote(rows.at[1], rows.at[2 * c], tile_send.at[2], tile_recv.at[2], sib)
    def plane_copy(slot, which, step):
        ref = rows.at[slot, y]
        return remote(
            ref, ref, plane_send.at[which, step], plane_recv.at[which, step], device(2 * others[step] + c, n)
        )

    def plane_land(slot, which, step):
        ref = rows.at[slot, others[YS - 2 - step]]
        return remote(ref, ref, plane_send.at[which, step], plane_recv.at[which, step], sib)

    swap_land = remote(rows.at[1], rows.at[2 - 2 * c], tile_send.at[2], tile_recv.at[2], sib)

    before(-START, 1 - CONV_AHEAD[0])

    @pl.when(native)
    def _():
        feat_local.start()
        own_local.start()

    @pl.when(jnp.logical_not(native))
    def _():
        feat_copy.start()
        own_copy.start()

    @pl.when(outer_native)
    def _():
        outer_local.start()

    @pl.when(both(out_valid, jnp.logical_not(outer_native)))
    def _():
        outer_copy.start()

    before(1 - CONV_AHEAD[0], 1 - CONV_AHEAD[1])

    @pl.when(jnp.logical_not(native))
    def _():
        own_copy.wait_recv()
        for step in range(YS - 1):
            plane_copy(1, 0, step).start()

    @pl.when(both(in_valid, jnp.logical_not(outer_native)))
    def _():
        outer_land.wait_recv()
        for step in range(YS - 1):
            plane_copy(2 * c, 1, step).start()

    before(1 - CONV_AHEAD[1], 1 - CONV_AHEAD[2])

    def halo(l, t, which):
        own = hb.at[l, t, 2]
        if which == 0:
            return remote(own, hb.at[l, t, c], halo_send.at[l, t, 0], halo_recv.at[l, t, c], right)
        if which == 1:
            return remote(own, hb.at[l, t, c + 3], halo_send.at[l, t, 1], halo_recv.at[l, t, c], left)
        if which == 2:
            return remote(own, hb.at[l, t, 1 + 2 * c], halo_send.at[l, t, 2], halo_recv.at[l, t, 2], sib)
        return remote(
            hb.at[l, t, 1 + 2 * c], hb.at[l, t, 4 * c], halo_send.at[l, t, 3], halo_recv.at[l, t, 3], sib
        )

    def landed(l, t, slot, which):
        ref = hb.at[l, t, slot]
        remote(ref, ref, halo_send.at[l, t, 3], halo_recv.at[l, t, which], sib).wait_recv()

    def send_halo(l, t):
        @pl.when(both(has_right, c == 1))
        def _():
            halo(l, t, 0).start()

        @pl.when(has_left)
        def _():
            halo(l, t, 1).start()

        @pl.when(both(has_right, c == 0))
        def _():
            halo(l, t, 0).start()

        halo(l, t, 2).start()

    def convolve(l, t):
        now = xs[2 + t]
        before = xs[1 + t - lax.rem(l, 2)]
        pre = jnp.dot(
            jnp.concatenate([before, now], axis=1), wc[l].reshape(2 * ch, 2 * ch), preferred_element_type=F32
        )
        gate = 0.5 * jnp.tanh(0.5 * pre[:, ch:]) + 0.5
        hb[l, t, 2] = (jnp.tanh(pre[:, :ch]) * gate).astype(BF16)

    @pl.when(native)
    def _():
        feat_local.wait()

    @pl.when(jnp.logical_not(native))
    def _():
        feat_copy.wait_recv()

    need(0, 0)
    for t in range(steps):
        convolve(0, t)
        send_halo(0, t)

    @pl.when(native)
    def _():
        own_local.wait()

    @pl.when(jnp.logical_not(native))
    def _():
        for step in range(YS - 1):
            plane_land(1, 0, step).wait_recv()

    swap_copy.start()

    @pl.when(outer_native)
    def _():
        outer_local.wait()

    @pl.when(both(in_valid, jnp.logical_not(outer_native)))
    def _():
        for step in range(YS - 1):
            plane_land(2 * c, 1, step).wait_recv()

    before(1 - CONV_AHEAD[2], 0)
    swap_land.wait_recv()
    for e in range(2):
        mid = rows[1, :, e].reshape(tile, 3 * tile)
        for col in range(5):
            inside = mid[:, (col - 1) * tile : col * tile] if 0 < col < 4 else jnp.zeros((tile, tile), BF16)
            hops[col, e * tile : (e + 1) * tile] = inside
        for col in range(5):
            total = jnp.zeros((tile, tile), F32)
            for via in range(3):
                if 0 <= col - via < 3:
                    total = total + jnp.dot(
                        mid[:, via * tile : (via + 1) * tile],
                        rows[via, :, e, :, (col - via) * tile : (col - via + 1) * tile].reshape(tile, tile),
                        preferred_element_type=F32,
                    )
            hops[col, (2 + e) * tile : (3 + e) * tile] = total.astype(BF16)
    for i in range(4):
        near_hops[:, i * tile : (i + 1) * tile] = hops[c + i]
    far_hops[...] = hops[4 - 4 * c, 2 * tile :]

    def hand_on(l, t):
        @pl.when(outer_ok)
        def _():
            landed(l, t, 1 + 2 * c, 1 - c)
            halo(l, t, 3).start()

    def out_copy(section, t):
        return remote(
            obuf.at[t, section],
            out.at[m, t],
            out_send.at[section, t],
            out_recv.at[m, t],
            device(section, r),
        )

    def out_local(section, t, sample):
        return pltpu.make_async_copy(obuf.at[t, section], out.at[sample, t], out_recv.at[sample, t])

    def finish(t):
        if t == 0:
            need(last_layer, 1)
        result = tot[t * tile : (t + 1) * tile] + jnp.dot(
            hb[last_layer, t, 2], wm[last_layer, 0:4].reshape(ch, ch), preferred_element_type=F32
        )
        obuf[t] = result.astype(BF16).reshape(layers, tile // layers, ch)
        for section in range(layers):
            keep = both(at_home, s == section)

            @pl.when(keep)
            def _():
                out_local(section, t, m).start()

            @pl.when(jnp.logical_not(keep))
            def _():
                out_copy(section, t).start()

    @pl.loop(0, last_layer)
    def _(l):
        need(l, 1)
        own = hb[l, :, 2].reshape(steps * tile, ch)
        tot[...] += jnp.dot(own, wm[l, 0:4].reshape(ch, ch), preferred_element_type=F32)
        base[...] = xs[2:].reshape(steps * tile, ch).astype(F32) + jnp.dot(
            own, wm[l, 4:8].reshape(ch, ch), preferred_element_type=F32
        )
        hand_on(l, 0)
        for t in range(steps):
            landed(l, t, 3 - 2 * c, 2)

            @pl.when(outer_ok)
            def _():
                landed(l, t, 4 * c, c)

            fields = jnp.dot(
                near_hops[...], hb[l, t, pl.ds(c, 4)].reshape(4 * tile, ch), preferred_element_type=F32
            ).astype(BF16)
            wide = jnp.concatenate([fields[i * tile : (i + 1) * tile] for i in range(4)], axis=1)
            mixed = base[t * tile : (t + 1) * tile] + jnp.dot(
                wide, wm[l, 8:24].reshape(4 * ch, ch), preferred_element_type=F32
            )
            point(l, t)

            @pl.when(inner_ok)
            def _():
                landed(l, t, 4 - 4 * c, 3)

            if t < steps - 1:
                hand_on(l, t + 1)

            fields = jnp.dot(far_hops[...], hb[l, t, 4 - 4 * c], preferred_element_type=F32).astype(BF16)
            wide = jnp.concatenate([fields[:tile], fields[tile:]], axis=1)
            mixed = mixed + jnp.dot(wide, wm[l, 16:24].reshape(2 * ch, ch), preferred_element_type=F32)
            xs[2 + t] = mixed.astype(BF16)
            if t == 0:
                need(l + 1, 0)
            convolve(l + 1, t)

            @pl.when(l < last_layer - 1)
            def _():
                send_halo(l + 1, t)

            @pl.when(l == last_layer - 1)
            def _():
                finish(t)

    @pl.when(jnp.logical_not(native))
    def _():
        feat_copy.wait_send()
        own_copy.wait_send()
        for step in range(YS - 1):
            plane_copy(1, 0, step).wait_send()

    @pl.when(both(out_valid, jnp.logical_not(outer_native)))
    def _():
        outer_copy.wait_send()

    @pl.when(both(in_valid, jnp.logical_not(outer_native)))
    def _():
        for step in range(YS - 1):
            plane_copy(2 * c, 1, step).wait_send()

    swap_copy.wait_send()

    @pl.loop(0, last_layer)
    def _(l):
        for t in range(steps):
            @pl.when(has_right)
            def _():
                halo(l, t, 0).wait_send()

            @pl.when(has_left)
            def _():
                halo(l, t, 1).wait_send()

            halo(l, t, 2).wait_send()

            @pl.when(outer_ok)
            def _():
                halo(l, t, 3).wait_send()

        drain_weights(l)

    drain_weights(last_layer)

    for section in range(layers):
        @pl.when(jnp.logical_not(both(at_home, s == section)))
        def _():
            for t in range(steps):
                out_copy(section, t).wait_send()

    for sample in range(layers):
        keep = both(at_home, m == sample)

        @pl.when(keep)
        def _():
            for t in range(steps):
                out_local(s, t, sample).wait()

        @pl.when(jnp.logical_not(keep))
        def _():
            for t in range(steps):
                ref = out.at[sample, t]
                remote(obuf.at[t, 0], ref, out_send.at[sample, t], out_recv.at[sample, t], sib).wait_recv()


def body(
    features_in,
    filter_gate,
    self_mix,
    hop_one_mix,
    hop_two_mix,
    skip_weight,
    tile_values,
    tile_columns,
    tile_counts,
):
    micro, tile, steps, ch = features_in.shape
    layers = lax.axis_size("section")
    blocks = lax.axis_size("node")
    part = ch // 4
    feat = features_in.transpose(0, 2, 1, 3)
    dma = pltpu.SemaphoreType.DMA
    in_hbm = pl.BlockSpec(memory_space=pltpu.HBM)
    in_vmem = pl.BlockSpec(memory_space=pltpu.VMEM)
    in_smem = pl.BlockSpec(memory_space=pltpu.SMEM)
    landed = pl.pallas_call(
        functools.partial(kernel, layers, blocks),
        out_shape=jax.ShapeDtypeStruct((micro, steps, tile // layers, ch), BF16),
        in_specs=[in_hbm] * 6 + [in_vmem, in_smem, in_smem],
        out_specs=in_hbm,
        scratch_shapes=[
            pltpu.VMEM((2 + steps, tile, ch), BF16),
            pltpu.VMEM((layers, steps, 5, tile, ch), BF16),
            pltpu.VMEM((layers, 8, ch // 4, 2 * ch), BF16),
            pltpu.VMEM((layers, 24, part, ch), BF16),
            pltpu.VMEM((YS, 2, tile // YS, 3 * tile), BF16),
            pltpu.VMEM((3, YS, 2, tile // YS, 3 * tile), BF16),
            pltpu.VMEM((5, 4 * tile, tile), BF16),
            pltpu.VMEM((4 * tile, 4 * tile), BF16),
            pltpu.VMEM((2 * tile, tile), BF16),
            pltpu.VMEM((steps * tile, ch), F32),
            pltpu.VMEM((steps * tile, ch), F32),
            pltpu.VMEM((steps, layers, tile // layers, ch), BF16),
            dma((5,)),
            dma((2,)),
            dma((3,)),
            dma((3,)),
            dma((2, 3)),
            dma((2, 3)),
            dma((layers - 1, steps, 4)),
            dma((layers - 1, steps, 4)),
            dma((layers, 2, 7)),
            dma((layers, 2)),
            dma((layers, 2, 3)),
            dma((layers, 2)),
            dma((layers, steps)),
            dma((layers, steps)),
        ],
        compiler_params=pltpu.CompilerParams(
            collective_id=0, has_side_effects=True, vmem_limit_bytes=62 * 1024 * 1024
        ),
        cost_estimate=pl.CostEstimate(flops=7_000_000_000, bytes_accessed=4_000_000, transcendentals=3_000_000),
    )(
        feat,
        filter_gate.reshape(8, ch // 4, 2 * ch),
        self_mix.reshape(4, part, ch),
        hop_one_mix.reshape(8, part, ch),
        hop_two_mix.reshape(8, part, ch),
        skip_weight.reshape(4, part, ch),
        tile_values[:, 0],
        tile_columns[:, 0],
        tile_counts[:, 0],
    )
    return landed.transpose(0, 2, 1, 3).astype(F32)[:, None]


def solution(mesh):
    in_specs = (
        P(None, "node", None, None),
        P("section", None, None, None),
        P("section", None, None),
        P("section", None, None, None),
        P("section", None, None, None),
        P("section", None, None),
        P(None, "node", None, None, None),
        P(None, "node", None),
        P(None, "node"),
    )
    out_specs = P(None, "node", "section", None, None)
    return jax.shard_map(body, mesh=mesh, in_specs=in_specs, out_specs=out_specs, check_vma=False)
```
